32 devices in a mesh: grp: 2 (over y), slab: 4 (over z), blk: 2 (over x), sub: 2 (over core).
Axes of the slice: x: 2, y: 2, z: 4, core: 2. Of those that a mesh axis runs over, the one named last changes fastest.
Arguments:
- cell_x: int32 [8192], P(('grp', 'slab', 'blk', 'sub')), parts along dimension 0, may hold values from 0 to 63
- cell_y: int32 [8192], P(('grp', 'slab', 'blk', 'sub')), parts along dimension 0, may hold values from 0 to 127
- cell_z: int32 [8192], P(('grp', 'slab', 'blk', 'sub')), parts along dimension 0, may hold values from 0 to 127
- offsets: float32 [3, 8192], P(None, ('grp', 'slab', 'blk', 'sub')), parts along dimension 1, may hold values from 0 to 1
- charge: float32 [8192], P(('grp', 'slab', 'blk', 'sub')), parts along dimension 0, may hold values from -4 to 4
- block_count: int32 [32], P(('grp', 'slab', 'blk', 'sub')), parts along dimension 0, may hold values from 0 to 256, as said below
- level_amplitude: float32 [4], replicated, may hold values from 0.5 to 2
- density: float32 [512, 256, 256], P(('grp', 'slab'), 'blk', 'sub'), parts along dimension 0, may hold values from 0.3 to 8.2
Outputs:
- field: float32 [512, 256, 256], P(('grp', 'slab'), 'blk', 'sub'), parts along dimension 0
- energy: float32 [2], P('grp'), parts along dimension 0
The draws below stay inside these ranges and needn't reach their ends.
There are 2 independent parts, one for each index of `grp`. The reference program is written for one: setup_inputs(seed, part) draws one part's arguments, and reference() takes and returns one part's arrays. A program takes and returns all parts, laid end to end along the dimension named above; an argument that names none is the same for every part. Nothing has to cross between parts.
Inputs may be any that keep to these rules, and one draw needn't show every extreme that they name: `block_count`: within the 1 block of each device, blocks with a nonzero count come before blocks with count 0; some device has every block full.
All inputs are finite; a program needn't handle non-finite values.
Results may differ from the reference program's by a relative error of at most 0.0021.
Values sent between devices are 32-bit elements; how exact they have to be, the bound alone decides.
No kernel may reach another device: no remote copies, remote signals or barrier semaphores. Data moves between devices by JAX's collectives and lax.ppermute only.
A program may use at most 64 MiB of HBM per device.

```python
import math
import jax
import jax.numpy as jnp
from jax import lax

G0X = 64
G0Y = 128
G0Z = 128
FINE_X = 256
FINE_Y = 256
FINE_Z = 256
BQ = 256
BLK_DEV = 1
SLOTS = 4096
NBLOCKS = 16


def draw_block_count(key, part):
    devices_part = NBLOCKS // BLK_DEV
    key_used = jax.random.fold_in(key, 11)
    key_counts = jax.random.fold_in(key, 12)
    key_full = jax.random.fold_in(key, 13)
    used = jax.random.randint(key_used, (devices_part, 1), max(1, BLK_DEV - 1), BLK_DEV + 1)
    counts = jax.random.randint(key_counts, (devices_part, BLK_DEV), BQ // 2, BQ + 1)
    busiest = jax.random.randint(key_full, (), 0, devices_part)
    columns = jnp.arange(BLK_DEV, dtype=jnp.int32)[None, :]
    counts = jnp.where(columns < used, counts, 0)
    counts = jnp.where(jnp.arange(devices_part, dtype=jnp.int32)[:, None] == busiest, BQ, counts)
    return counts.reshape(-1).astype(jnp.int32)


def draw_density(key, part):
    positions = jnp.arange(FINE_X, dtype=jnp.float32)[:, None, None]
    rising = 1.0 + 2.0 * positions / (FINE_X - 1)
    base = jnp.exp(jax.random.uniform(jax.random.fold_in(key, 22), (FINE_X, FINE_Y, FINE_Z), jnp.float32, -1.0, 1.0))
    return (base * rising).astype(jnp.float32)


def set_ends(drawn, rng, smallest, largest):
    longest = drawn.shape.index(max(drawn.shape))
    spots = []
    for shift in (0, 1):
        where = [jax.random.randint(jax.random.fold_in(rng, axis), (), 0, length) for axis, length in enumerate(drawn.shape)]
        where[longest] = (where[longest] + shift) % drawn.shape[longest]
        spots.append(tuple(where))
    return drawn.at[spots[0]].set(smallest).at[spots[1]].set(largest)


def shard_levels(own_key, dims, pieces, smallest, largest):
    level = 1.0
    for axis_at, blocks in pieces:
        draws = jax.random.uniform(jax.random.fold_in(jax.random.fold_in(own_key, 6), axis_at), (blocks,), jnp.float32, smallest / len(pieces), largest / len(pieces))
        level = level * jnp.repeat(jnp.exp(draws), dims[axis_at] // blocks).reshape((-1,) + (1,) * (len(dims) - 1 - axis_at))
    return level


def noise(own_key, extent, scale, most, cuts=(), kind=jnp.bfloat16):
    array = scale * jax.random.normal(own_key, extent, jnp.float32)
    if cuts:
        array = array * shard_levels(own_key, extent, cuts, -0.22, 0.18)
    return jnp.clip(array, -most, most).astype(kind)


def setup_inputs(seed: int = 0, part: int = 0) -> dict:
    keys = jax.random.split(jax.random.key(seed), 9)
    part_keys = jax.random.split(jax.random.fold_in(keys[8], part), 9)
    return {
        "cell_x": set_ends(jax.random.randint(part_keys[0], (SLOTS,), 0, G0X), jax.random.fold_in(part_keys[0], 1), 0, G0X - 1).astype(jnp.int32),
        "cell_y": set_ends(jax.random.randint(part_keys[1], (SLOTS,), 0, G0Y), jax.random.fold_in(part_keys[1], 1), 0, G0Y - 1).astype(jnp.int32),
        "cell_z": set_ends(jax.random.randint(part_keys[2], (SLOTS,), 0, G0Z), jax.random.fold_in(part_keys[2], 1), 0, G0Z - 1).astype(jnp.int32),
        "offsets": jnp.clip(1.0 * jax.random.uniform(part_keys[3], (3, SLOTS), jnp.float32) ** shard_levels(part_keys[3], (3, SLOTS), ((1, 16),), -0.2, 0.2), 0.0, 1.0),
        "charge": noise(part_keys[4], (SLOTS,), 1.0, 4.0, ((0, 16),), jnp.float32),
        "block_count": draw_block_count(jax.random.fold_in(jax.random.fold_in(keys[8], part), 71), part),
        "level_amplitude": jnp.clip(jnp.exp(jax.random.uniform(keys[6], (4,), jnp.float32, math.log(0.5), math.log(2.0))), 0.5, 2.0),
        "density": draw_density(jax.random.fold_in(jax.random.fold_in(keys[8], part), 71), part),
    }


spread_width = 1.25


def axis_weights(cells, shifts, base, coarse):
    position = (cells.astype(jnp.float32) + shifts) * (coarse / base)
    nodes = jnp.arange(coarse, dtype=jnp.float32)
    distance = nodes[None, :] - position[:, None]
    distance = distance - coarse * jnp.floor(distance / coarse + 0.5)
    return jnp.exp(-0.5 * (distance / spread_width) ** 2)


def level_dims():
    return [(G0X * (4 - factor) // 4, G0Y * (4 - factor) // 4, G0Z * (4 - factor) // 4) for factor in range(4)]


def spread_block(weighted, cells_x, cells_y, cells_z, shifts):
    totals = []
    for dim_x, dim_y, dim_z in level_dims():
        along_x = axis_weights(cells_x, shifts[0], G0X, dim_x)
        along_y = axis_weights(cells_y, shifts[1], G0Y, dim_y)
        along_z = axis_weights(cells_z, shifts[2], G0Z, dim_z)
        planes = ((weighted[:, None] * along_x)[:, :, None] * along_y[:, None, :]).reshape(weighted.shape[0], dim_x * dim_y).astype(jnp.bfloat16)
        totals.append(lax.dot_general(planes, along_z.astype(jnp.bfloat16), (((0,), (0,)), ((), ())), preferred_element_type=jnp.float32))
    return totals


def hat_matrix(fine, coarse, first_row, rows):
    fine_rows = first_row + jnp.arange(rows, dtype=jnp.int32)
    nodes = jnp.arange(coarse, dtype=jnp.int32)
    period = coarse * fine
    moved = (nodes[None, :] * fine - fine_rows[:, None] * coarse) % period
    moved = jnp.where(moved * 2 >= period, moved - period, moved)
    distance = moved.astype(jnp.float32) / fine
    return jnp.maximum(0.0, 1.0 - jnp.abs(distance))


def interpolate(mat_x, mat_y, mat_z, cube):
    highest = lax.Precision.HIGHEST
    first = jnp.einsum('ax,xyz->ayz', mat_x, cube, precision=highest)
    second = jnp.einsum('by,ayz->abz', mat_y, first, precision=highest)
    return jnp.einsum('cz,abz->abc', mat_z, second, precision=highest)


def reference(cell_x, cell_y, cell_z, offsets, charge, block_count, level_amplitude, density):
    live = (jnp.arange(BQ, dtype=jnp.int32)[None, :] < block_count[:, None]).astype(jnp.float32)
    weighted = charge.reshape(NBLOCKS, BQ) * live
    inputs = (weighted, cell_x.reshape(NBLOCKS, BQ), cell_y.reshape(NBLOCKS, BQ), cell_z.reshape(NBLOCKS, BQ), jnp.transpose(offsets.reshape(3, NBLOCKS, BQ), (1, 0, 2)))
    start = [jnp.zeros((dim_x * dim_y, dim_z), jnp.float32) for dim_x, dim_y, dim_z in level_dims()]

    def advance(totals, item):
        parts = spread_block(*item)
        return [total + part for total, part in zip(totals, parts)], None

    coarse, _ = lax.scan(advance, start, inputs)
    field = jnp.zeros((FINE_X, FINE_Y, FINE_Z), jnp.float32)
    for factor, (dim_x, dim_y, dim_z) in enumerate(level_dims()):
        cube = coarse[factor].reshape(dim_x, dim_y, dim_z)
        mat_x = hat_matrix(FINE_X, dim_x, 0, FINE_X)
        mat_y = hat_matrix(FINE_Y, dim_y, 0, FINE_Y)
        mat_z = hat_matrix(FINE_Z, dim_z, 0, FINE_Z)
        field = field + level_amplitude[factor] * interpolate(mat_x, mat_y, mat_z, cube)
    energy = (jnp.sum(density * field) / (FINE_X * FINE_Y * FINE_Z)).reshape(1)
    return field, energy
```

```python
import math
from fractions import Fraction

import jax
import jax.numpy as jnp
from jax import lax
from jax.experimental import pallas as pl
from jax.experimental.pallas import tpu as pltpu
from jax.sharding import PartitionSpec as P

G0X = 64
G0Y = 128
G0Z = 128
BQ = 256
LEVELS = 4

spread_width = 1.25
exponent = -0.5 / spread_width**2 * math.log2(math.e)


def round_up(value, unit):
    return -(-value // unit) * unit


class Plan:
    def __init__(self, fine, rows, slots):
        self.fine = fine
        self.rows = rows
        self.dims = [
            tuple(base * (LEVELS - level) // LEVELS for base in (G0X, G0Y, G0Z))
            for level in range(LEVELS)
        ]
        self.cells = [
            tuple(dim * part // whole for dim, part, whole in zip(dims, rows, fine))
            for dims in self.dims
        ]
        self.nodes = [tuple(count + 1 for count in cells) for cells in self.cells]
        self.pad_x = [round_up(nodes[0], 8) for nodes in self.nodes]
        self.pad_y = [round_up(nodes[1], 8) for nodes in self.nodes]
        self.pad_z = [round_up(nodes[2], 8) for nodes in self.nodes]
        self.off_wx = [sum(self.pad_x[:level]) for level in range(LEVELS + 1)]
        self.off_y = [sum(self.pad_y[:level]) for level in range(LEVELS + 1)]
        self.pairs = [round_up(nodes[0], 2) // 2 for nodes in self.nodes]
        self.plane_rows = [
            2 * pairs * pad for pairs, pad in zip(self.pairs, self.pad_y)
        ]
        self.off_s = [sum(self.plane_rows[:level]) for level in range(LEVELS + 1)]
        self.groups = [(0, 1), (2, 3)]
        self.off_z = [0, self.pad_z[0], 0, self.pad_z[2]]
        self.wide = [
            round_up(self.pad_z[a] + self.pad_z[b], 128) for a, b in self.groups
        ]
        self.width = max(self.wide)


def weights(position, first, dim, base, rows):
    place = position * (dim / base)
    nodes = first + lax.broadcasted_iota(jnp.int32, (rows, 1), 0).astype(jnp.float32)
    apart = jnp.abs(nodes - place)
    apart = jnp.minimum(apart, dim - apart)
    return jnp.exp2(apart * apart * exponent)


def spread_kernel(plan, starts, charges, grids, along_x, along_y, planes):
    begin = [starts[axis].astype(jnp.float32) for axis in range(3)]
    grids[...] = jnp.zeros_like(grids)

    def one_block(number, _):
        block = charges[number]
        weighted, place_x, place_y, place_z = (block[row : row + 1] for row in range(4))
        columns = []
        for level in range(LEVELS):
            dims, cells = plan.dims[level], plan.cells[level]
            off, pad = plan.off_wx[level], plan.pad_x[level]
            along_x[off : off + pad] = weighted * weights(
                place_x, begin[0] * cells[0], dims[0], G0X, pad
            )
            off, pad = plan.off_y[level], plan.pad_y[level]
            along_y[off : off + pad] = weights(
                place_y, begin[1] * cells[1], dims[1], G0Y, pad
            )
            columns.append(
                weights(
                    place_z, begin[2] * cells[2], dims[2], G0Z, plan.pad_z[level]
                )
            )
        for (low, high), wide in zip(plan.groups, plan.wide):
            parts = [columns[low], columns[high]]
            rest = wide - plan.pad_z[low] - plan.pad_z[high]
            if rest:
                parts.append(jnp.zeros((rest, BQ), jnp.float32))
            along_z = jnp.concatenate(parts, axis=0).astype(jnp.bfloat16)
            for level in (low, high):
                pad = plan.pad_y[level]
                off = plan.off_s[level]
                fixed = along_y[plan.off_y[level] : plan.off_y[level] + pad]
                for pair in range(plan.pairs[level]):
                    node = plan.off_wx[level] + 2 * pair
                    both = jnp.concatenate(
                        [
                            along_x[node : node + 1] * fixed,
                            along_x[node + 1 : node + 2] * fixed,
                        ],
                        axis=0,
                    )
                    planes[off + 2 * pair * pad : off + 2 * (pair + 1) * pad] = (
                        both.astype(jnp.bfloat16)
                    )
                rows = slice(off, off + plan.plane_rows[level])
                grids[rows, :wide] += lax.dot_general(
                    planes[rows],
                    along_z,
                    (((1,), (1,)), ((), ())),
                    preferred_element_type=jnp.float32,
                )
        return 0

    lax.fori_loop(0, charges.shape[0], one_block, 0)


def split(value):
    high = value.astype(jnp.bfloat16)
    return high, (value - high.astype(jnp.float32)).astype(jnp.bfloat16)


def field_kernel(plan, steps, amplitude, grids, hat_y, hat_z, density, field, energy, drawn):
    step = pl.program_id(0)
    rows_x, rows_y, rows_z = plan.rows

    @pl.when(step == 0)
    def _():
        for level in range(LEVELS):
            wide = plan.wide[level // 2]
            rows = slice(plan.off_s[level], plan.off_s[level + 1])
            high, low = split(grids[rows, :wide] * amplitude[level])
            drawn[rows] = jnp.dot(
                high, hat_z[level, :wide], preferred_element_type=jnp.float32
            ) + jnp.dot(low, hat_z[level, :wide], preferred_element_type=jnp.float32)
        energy[...] = jnp.zeros_like(energy)

    count = rows_x // steps
    total = jnp.zeros(energy.shape, jnp.float32)
    for plane in range(count):
        parts = []
        for level in range(LEVELS):
            cells = plan.cells[level][0]
            place = Fraction(plane * cells, rows_x)
            node = int(place)
            part = float(place - node)
            pad = plan.pad_y[level]
            first = plan.off_s[level] + step * (cells // steps * pad) + node * pad
            value = drawn[pl.ds(pl.multiple_of(first, 8), pad)]
            if part:
                second = drawn[pl.ds(pl.multiple_of(first + pad, 8), pad)]
                value = value * (1.0 - part) + second * part
            parts.append(value)
        high, low = split(jnp.concatenate(parts, axis=0))
        value = jnp.dot(hat_y[...], high, preferred_element_type=jnp.float32) + jnp.dot(
            hat_y[...], low, preferred_element_type=jnp.float32
        )
        field[plane] = value
        value = value * density[plane]
        total += jnp.sum(value.reshape(-1, 8, rows_z), axis=0)
    energy[...] += total


def hat_columns(rows, cells, height):
    row_ids = jnp.arange(rows, dtype=jnp.int32)
    col_ids = jnp.arange(height, dtype=jnp.int32)
    moved = col_ids[None, :] * rows - row_ids[:, None] * cells
    return jnp.maximum(0.0, 1.0 - jnp.abs(moved.astype(jnp.float32) / rows))


def butterfly(value, axes, join):
    for axis in axes:
        peers = lax.axis_size(axis)
        by = 1
        while by < peers:
            pairs = [(i, i ^ by) for i in range(peers)]
            value = join(value, lax.ppermute(value, axis, pairs))
            by *= 2
    return value


def on_device(cell_x, cell_y, cell_z, offsets, charge, block_count, level_amplitude, density):
    blocks = block_count.shape[0]
    rows = density.shape
    axes = ("slab", "blk", "sub")
    fine = tuple(count * lax.axis_size(axis) for count, axis in zip(rows, axes))
    plan = Plan(fine, rows, blocks)
    order = ("sub", "blk", "slab")

    live = jnp.arange(BQ, dtype=jnp.int32)[None, :] < block_count[:, None]
    weighted = charge.reshape(blocks, BQ) * live.astype(jnp.float32)
    mine = jnp.stack(
        [weighted]
        + [
            (cells.astype(jnp.float32) + shift).reshape(blocks, BQ)
            for cells, shift in zip((cell_x, cell_y, cell_z), offsets)
        ],
        axis=1,
    )
    charges = butterfly(mine, order, lambda a, b: jnp.concatenate([a, b], axis=0))

    starts = jnp.stack([lax.axis_index(axis) for axis in axes]).astype(jnp.int32)
    total_rows = plan.off_s[-1]
    smem = pl.BlockSpec(memory_space=pltpu.SMEM)
    vmem = pl.BlockSpec(memory_space=pltpu.VMEM)
    grids = pl.pallas_call(
        lambda *refs: spread_kernel(plan, *refs),
        out_shape=jax.ShapeDtypeStruct((total_rows, plan.width), jnp.float32),
        in_specs=[smem, vmem],
        out_specs=vmem,
        scratch_shapes=[
            pltpu.VMEM((plan.off_wx[-1], BQ), jnp.float32),
            pltpu.VMEM((plan.off_y[-1], BQ), jnp.float32),
            pltpu.VMEM((total_rows, BQ), jnp.bfloat16),
        ],
        compiler_params=pltpu.CompilerParams(vmem_limit_bytes=40 * 2**20),
        name="spread",
    )(starts, charges)

    hat_y = jnp.concatenate(
        [
            hat_columns(rows[1], plan.cells[level][1], plan.pad_y[level])
            for level in range(LEVELS)
        ],
        axis=1,
    ).astype(jnp.bfloat16)
    hat_z = []
    for level in range(LEVELS):
        hat = hat_columns(rows[2], plan.cells[level][2], plan.pad_z[level]).T
        before = plan.off_z[level]
        after = plan.width - before - plan.pad_z[level]
        hat_z.append(jnp.pad(hat, ((before, after), (0, 0))))
    hat_z = jnp.stack(hat_z).astype(jnp.bfloat16)

    steps = math.gcd(4, *(cells[0] for cells in plan.cells))
    block = (rows[0] // steps, rows[1], rows[2])
    field, energy = pl.pallas_call(
        lambda *refs: field_kernel(plan, steps, *refs),
        grid=(steps,),
        out_shape=(
            jax.ShapeDtypeStruct(rows, jnp.float32),
            jax.ShapeDtypeStruct((8, rows[2]), jnp.float32),
        ),
        in_specs=[
            smem,
            pl.BlockSpec((total_rows, plan.width), lambda i: (0, 0)),
            pl.BlockSpec(hat_y.shape, lambda i: (0, 0)),
            pl.BlockSpec(hat_z.shape, lambda i: (0, 0, 0)),
            pl.BlockSpec(block, lambda i: (i, 0, 0)),
        ],
        out_specs=(
            pl.BlockSpec(block, lambda i: (i, 0, 0)),
            pl.BlockSpec((8, rows[2]), lambda i: (0, 0)),
        ),
        scratch_shapes=[pltpu.VMEM((total_rows, rows[2]), jnp.float32)],
        compiler_params=pltpu.CompilerParams(vmem_limit_bytes=40 * 2**20),
        name="field",
    )(level_amplitude, grids, hat_y, hat_z, density)

    energy = butterfly(energy, order, lambda a, b: a + b)
    energy = jnp.sum(energy) / math.prod(fine)
    return field, energy.reshape(1)


def solution(mesh):
    split_all = ("grp", "slab", "blk", "sub")
    in_specs = (
        P(split_all),
        P(split_all),
        P(split_all),
        P(None, split_all),
        P(split_all),
        P(split_all),
        P(),
        P(("grp", "slab"), "blk", "sub"),
    )
    out_specs = (P(("grp", "slab"), "blk", "sub"), P("grp"))
    return jax.shard_map(
        on_device, mesh=mesh, in_specs=in_specs, out_specs=out_specs, check_vma=False
    )
```

```python
import math
from fractions import Fraction

import jax
import jax.numpy as jnp
from jax import lax
from jax.experimental import pallas as pl
from jax.experimental.pallas import tpu as pltpu
from jax.sharding import PartitionSpec as P

G0X = 64
G0Y = 128
G0Z = 128
BQ = 256
LEVELS = 4
GROUPS = ((0, 1), (2, 3))

spread_width = 1.25
exponent = -0.5 / spread_width**2 * math.log2(math.e)

vmem = pl.BlockSpec(memory_space=pltpu.VMEM)
smem = pl.BlockSpec(memory_space=pltpu.SMEM)
hbm = pl.BlockSpec(memory_space=pltpu.HBM)
params = pltpu.CompilerParams(vmem_limit_bytes=48 * 2**20)


def round_up(value, unit):
    return -(-value // unit) * unit


class Plan:
    def __init__(self, fine, rows):
        self.rows = rows
        self.dims = [
            tuple(base * (LEVELS - level) // LEVELS for base in (G0X, G0Y, G0Z))
            for level in range(LEVELS)
        ]
        self.cells = [
            tuple(dim * part // whole for dim, part, whole in zip(dims, rows, fine))
            for dims in self.dims
        ]
        self.nodes_x = [cells[0] + 1 for cells in self.cells]
        self.main_y = [round_up(cells[1], 16) for cells in self.cells]
        self.pad_x = [round_up(cells[0] + 1, 8) for cells in self.cells]
        self.pad_y = [
            max(main, round_up(cells[1] + 1, 8))
            for main, cells in zip(self.main_y, self.cells)
        ]
        self.pad_z = [round_up(cells[2] + 1, 8) for cells in self.cells]
        self.off_x = [sum(self.pad_x[:level]) for level in range(LEVELS + 1)]
        self.off_y = [sum(self.pad_y[:level]) for level in range(LEVELS + 1)]
        self.off_main = [0]
        for level in range(LEVELS):
            self.off_main.append(
                self.off_main[-1] + self.nodes_x[level] * self.main_y[level]
            )
        self.main_rows = self.off_main[-1]
        self.edge_rows = [
            round_up(self.pad_x[a] + self.pad_x[b], 16) for a, b in GROUPS
        ]
        self.off_edge = []
        at = self.main_rows
        for (a, b), count in zip(GROUPS, self.edge_rows):
            self.off_edge += [at, at + self.pad_x[a]]
            at += count
        self.total = at
        self.off_z = [0, self.pad_z[0], 0, self.pad_z[2]]
        self.width = max(
            round_up(self.pad_z[a] + self.pad_z[b], 128) for a, b in GROUPS
        )
        self.off_stack = [sum(self.main_y[:level]) for level in range(LEVELS + 1)]
        self.stack = round_up(self.off_stack[-1] + 8, 16)

    def main(self, level, node=0, count=1):
        pad = self.main_y[level]
        first = self.off_main[level] + node * pad
        return slice(first, first + count * pad)


def split(value):
    high = value.astype(jnp.bfloat16)
    return high, (value - high.astype(jnp.float32)).astype(jnp.bfloat16)


def dot(left, right, transposed=False):
    return lax.dot_general(
        left,
        right,
        (((1,), (1 if transposed else 0,)), ((), ())),
        preferred_element_type=jnp.float32,
    )


def hat(shape, fine_dim, rows, cells, shift, last):
    point = lax.broadcasted_iota(jnp.int32, shape, fine_dim)
    node = lax.broadcasted_iota(jnp.int32, shape, 1 - fine_dim) - shift
    apart = (node * rows - point * cells).astype(jnp.float32) / rows
    value = jnp.maximum(0.0, 1.0 - jnp.abs(apart))
    return jnp.where((node >= 0) & (node <= last), value, 0.0)


def edge_hat(plan, shape, row_dim):
    row = lax.broadcasted_iota(jnp.int32, shape, row_dim)
    column = lax.broadcasted_iota(jnp.int32, shape, 1 - row_dim)
    value = jnp.zeros(shape, jnp.float32)
    for level in range(LEVELS):
        cells = plan.cells[level][0]
        node = column - (plan.off_edge[level] - plan.main_rows)
        apart = (node * plan.rows[0] - (row >> 3) * cells).astype(jnp.float32)
        one = jnp.maximum(0.0, 1.0 - jnp.abs(apart / plan.rows[0]))
        here = ((row & 7) == level) & (node >= 0) & (node <= cells)
        value = jnp.where(here, one, value)
    return value


def hats_kernel(plan, hat_y, hat_y_turned, hat_z, hat_z_turned, hat_x, hat_x_turned):
    _, rows_y, rows_z = plan.rows
    for turned in (False, True):
        fine_dim = 1 if turned else 0
        parts = []
        edge = 0.0
        for level in range(LEVELS):
            cells = plan.cells[level]
            shape = (rows_y, plan.main_y[level])
            parts.append(
                hat(
                    shape[::-1] if turned else shape, fine_dim, rows_y, cells[1], 0, cells[1] - 1
                )
            )
            shape = (rows_y, plan.stack - plan.off_stack[-1])
            shape = shape[::-1] if turned else shape
            one = hat(shape, fine_dim, rows_y, cells[1], level - cells[1], cells[1])
            column = lax.broadcasted_iota(jnp.int32, shape, 1 - fine_dim)
            edge = edge + jnp.where(column == level, one, 0.0)
            shape = (rows_z, plan.width)
            one = hat(
                shape[::-1] if not turned else shape,
                0 if turned else 1,
                rows_z,
                cells[2],
                plan.off_z[level],
                cells[2],
            ).astype(jnp.bfloat16)
            (hat_z_turned if turned else hat_z)[level] = jnp.concatenate([one, one], axis=0)
        whole = jnp.concatenate(parts + [edge], axis=1 - fine_dim).astype(jnp.bfloat16)
        if turned:
            hat_y_turned[...] = jnp.concatenate([whole, whole], axis=1)
        else:
            hat_y[...] = whole
    hat_x[...] = edge_hat(plan, hat_x.shape, 0).astype(jnp.bfloat16)
    hat_x_turned[...] = edge_hat(plan, hat_x_turned.shape, 1).astype(jnp.bfloat16)


def prepare_kernel(
    cell_x, cell_y, cell_z, offsets, charge, counts, amplitude, mine, scales,
    cells, shifts, held, levels, live, sems,
):
    blocks = mine.shape[0]
    copies = [
        pltpu.make_async_copy(source, target, sems.at[number])
        for number, (source, target) in enumerate(
            [
                (cell_x, cells.at[0]),
                (cell_y, cells.at[1]),
                (cell_z, cells.at[2]),
                (offsets, shifts),
                (charge, held),
                (counts, live),
                (amplitude, levels),
            ]
        )
    ]
    for copy in copies:
        copy.start()
    for copy in copies:
        copy.wait()
    slot = lax.broadcasted_iota(jnp.int32, (1, BQ), 1)
    for block in range(blocks):
        columns = slice(block * BQ, (block + 1) * BQ)
        mine[block, 0:1] = jnp.where(slot < live[block], held[:, columns], 0.0)
        for axis in range(3):
            mine[block, axis + 1 : axis + 2] = (
                cells[axis, :, columns].astype(jnp.float32) + shifts[axis : axis + 1, columns]
            )
    for level in range(LEVELS):
        scales[level : level + 1] = jnp.full((1, scales.shape[1]), levels[level], jnp.float32)
    scales[LEVELS:] = jnp.zeros((8 - LEVELS, scales.shape[1]), jnp.float32)


def weights(position, first, dim, base, rows):
    place = position * (dim / base)
    nodes = first + lax.broadcasted_iota(jnp.int32, (rows, 1), 0).astype(jnp.float32)
    apart = jnp.abs(nodes - place)
    apart = jnp.minimum(apart, dim - apart)
    return jnp.exp2(apart * apart * exponent)


def spread_kernel(plan, together, first, last, *refs):
    refs = list(refs)
    starts, charges = refs[:2]
    before = None if first else refs[2]
    turned = refs[2 if first else 3] if last else None
    outs = refs[2 + (not first) + last :]
    if last:
        energy = outs.pop(1)
    grids, along_x, along_y, along_z, planes = outs
    begin = [starts[axis].astype(jnp.float32) for axis in range(3)]
    steps = charges.shape[0] // together

    def one_step(step, before):
        for number in range(together):
            block = charges[step * together + number]
            columns = slice(number * BQ, (number + 1) * BQ)
            weighted, place_x, place_y, place_z = (block[row : row + 1] for row in range(4))
            for group, levels in enumerate(GROUPS):
                column_z = []
                for level in levels:
                    dims, cells = plan.dims[level], plan.cells[level]
                    along_x[plan.off_x[level] : plan.off_x[level + 1]] = weighted * weights(
                        place_x, begin[0] * cells[0], dims[0], G0X, plan.pad_x[level]
                    )
                    along_y[plan.off_y[level] : plan.off_y[level + 1]] = weights(
                        place_y, begin[1] * cells[1], dims[1], G0Y, plan.pad_y[level]
                    )
                    column_z.append(
                        weights(place_z, begin[2] * cells[2], dims[2], G0Z, plan.pad_z[level])
                    )
                rest = plan.width - sum(plan.pad_z[level] for level in levels)
                if rest:
                    column_z.append(jnp.zeros((rest, BQ), jnp.float32))
                along_z[group, :, columns] = jnp.concatenate(column_z, axis=0).astype(jnp.bfloat16)
                edges = []
                for level in levels:
                    fixed = along_y[plan.off_y[level] : plan.off_y[level] + plan.main_y[level]]
                    for node in range(plan.nodes_x[level]):
                        at = plan.off_x[level] + node
                        planes[plan.main(level, node), columns] = (
                            along_x[at : at + 1] * fixed
                        ).astype(jnp.bfloat16)
                    at = plan.off_y[level] + plan.cells[level][1]
                    edges.append(
                        along_x[plan.off_x[level] : plan.off_x[level + 1]] * along_y[at : at + 1]
                    )
                rest = plan.edge_rows[group] - sum(edge.shape[0] for edge in edges)
                if rest:
                    edges.append(jnp.zeros((rest, BQ), jnp.float32))
                at = plan.off_edge[levels[0]]
                planes[at : at + plan.edge_rows[group], columns] = jnp.concatenate(
                    edges, axis=0
                ).astype(jnp.bfloat16)
        for group, levels in enumerate(GROUPS):
            at = plan.off_edge[levels[0]]
            for rows in [plan.main(level, 0, plan.nodes_x[level]) for level in levels] + [
                slice(at, at + plan.edge_rows[group])
            ]:
                value = dot(planes[rows], along_z[group], transposed=True)
                grids[rows] = value if before is None else before[rows] + value

    one_step(0, before)
    if steps <= 2:
        for step in range(1, steps):
            one_step(step, grids)
    else:
        lax.fori_loop(1, steps, lambda step, _: one_step(step, grids), None)
    if last:
        rows = plan.total // 8
        energy[...] = jnp.sum(
            (grids[...] * turned[...]).reshape(rows, 8, plan.width), axis=0
        )


def hat_terms(points, cells):
    terms = []
    for point in range(points):
        place = Fraction(point * cells, points)
        node = int(place)
        part = float(place - node)
        terms.append([(node, 1.0 - part)] + ([(node + 1, part)] if part else []))
    return terms


def turned_kernel(
    plan, density, scales, hat_y_turned, hat_z_turned, hat_x_turned, unused, out,
    held, along_y, along_x, sems,
):
    rows_x = plan.rows[0]
    parts = sems.shape[0]
    count = rows_x // parts
    copies = [
        pltpu.make_async_copy(
            density.at[pl.ds(part * count, count)],
            held.at[pl.ds(part * count, count)],
            sems.at[part],
        )
        for part in range(parts)
    ]
    for copy in copies:
        copy.start()
    terms = [hat_terms(rows_x, cells[0]) for cells in plan.cells]
    for part in range(parts):
        copies[part].wait()
        for plane in range(part * count, (part + 1) * count, 2):
            both = jnp.concatenate([held[plane], held[plane + 1]], axis=1)
            value = dot(hat_y_turned[...], jnp.concatenate(split(both), axis=0))
            along_y[plane] = value[:, : plan.rows[2]]
            along_y[plane + 1] = value[:, plan.rows[2] :]
    for level in range(LEVELS):
        stack = slice(plan.off_stack[level], plan.off_stack[level + 1])
        for node in range(plan.nodes_x[level]):
            total = None
            for plane in range(rows_x):
                for at, part in terms[level][plane]:
                    if at == node:
                        value = along_y[plane, stack]
                        if part != 1.0:
                            value = value * part
                        total = value if total is None else total + value
            if total is None:
                total = jnp.zeros((plan.main_y[level], plan.rows[2]), jnp.float32)
            along_x[plan.main(level, node)] = total
    first = plan.off_stack[-1]
    edges = jnp.concatenate([along_y[plane, first : first + 8] for plane in range(rows_x)], axis=0)
    high, low = split(edges)
    along_x[plan.main_rows :] = dot(hat_x_turned[...], high) + dot(hat_x_turned[...], low)
    for level in range(LEVELS):
        edge = plan.off_edge[level]
        for rows in (
            plan.main(level, 0, plan.nodes_x[level]),
            slice(edge, edge + plan.pad_x[level]),
        ):
            value = jnp.concatenate(split(along_x[rows]), axis=1)
            out[rows] = dot(value, hat_z_turned[level]) * scales[level : level + 1, :1]
    for group, levels in enumerate(GROUPS):
        at = plan.off_edge[levels[1]] + plan.pad_x[levels[1]]
        end = plan.off_edge[levels[0]] + plan.edge_rows[group]
        if end > at:
            out[at:end] = jnp.zeros((end - at, plan.width), jnp.float32)


def field_kernel(plan, part, parts, *refs):
    grids, scales, hat_y, hat_z, hat_x = refs[:5]
    field, drawn = refs[-2:]
    rows_x = plan.rows[0]
    count = rows_x // parts
    planes = range(part * count, (part + 1) * count)
    terms = [hat_terms(rows_x, cells[0]) for cells in plan.cells]

    def interpolate_z(level, rows):
        value = jnp.concatenate(split(grids[rows] * scales[level : level + 1, : plan.width]), axis=1)
        drawn[rows] = dot(value, hat_z[level])

    for level in range(LEVELS):
        used = [node for plane in planes for node, _ in terms[level][plane]]
        interpolate_z(level, plan.main(level, min(used), max(used) - min(used) + 1))
        edge = plan.off_edge[level]
        interpolate_z(level, slice(edge, edge + plan.pad_x[level]))
    for group, levels in enumerate(GROUPS):
        at = plan.off_edge[levels[1]] + plan.pad_x[levels[1]]
        end = plan.off_edge[levels[0]] + plan.edge_rows[group]
        if end > at:
            drawn[at:end] = jnp.zeros((end - at, drawn.shape[1]), jnp.float32)
    high, low = split(drawn[plan.main_rows :])
    rows = slice(planes[0] * 8, (planes[-1] + 1) * 8)
    edges = dot(hat_x[rows], high) + dot(hat_x[rows], low)
    rest = plan.stack - plan.off_stack[-1] - 8
    for plane in planes[::2]:
        both = []
        for one in (plane, plane + 1):
            stack = []
            for level in range(LEVELS):
                total = None
                for node, weight in terms[level][one]:
                    value = drawn[plan.main(level, node)]
                    if weight != 1.0:
                        value = value * weight
                    total = value if total is None else total + value
                stack.append(total)
            at = (one - planes[0]) * 8
            stack.append(edges[at : at + 8])
            if rest:
                stack.append(jnp.zeros((rest, drawn.shape[1]), jnp.float32))
            both.append(jnp.concatenate(stack, axis=0))
        value = dot(hat_y[...], jnp.concatenate(both, axis=1).astype(jnp.bfloat16))
        field[plane - planes[0]] = value[:, : plan.rows[2]]
        field[plane + 1 - planes[0]] = value[:, plan.rows[2] :]


def rounds(order):
    for axis in order:
        peers = lax.axis_size(axis)
        by = 1
        while by < peers:
            yield axis, [(i, i ^ by) for i in range(peers)]
            by *= 2


def on_device(cell_x, cell_y, cell_z, offsets, charge, block_count, level_amplitude, density):
    blocks = block_count.shape[0]
    rows = density.shape
    axes = ("slab", "blk", "sub")
    plan = Plan(tuple(count * lax.axis_size(axis) for count, axis in zip(rows, axes)), rows)
    order = ("sub", "blk", "slab")
    steps = list(rounds(order))
    f32, bf16 = jnp.float32, jnp.bfloat16

    hats = pl.pallas_call(
        lambda *refs: hats_kernel(plan, *refs),
        out_shape=[
            jax.ShapeDtypeStruct(shape, bf16)
            for shape in (
                (rows[1], plan.stack),
                (plan.stack, 2 * rows[1]),
                (LEVELS, 2 * plan.width, rows[2]),
                (LEVELS, 2 * rows[2], plan.width),
                (rows[0] * 8, plan.total - plan.main_rows),
                (plan.total - plan.main_rows, rows[0] * 8),
            )
        ],
        out_specs=[vmem] * 6,
        compiler_params=params,
        name="hats",
    )()
    hat_y, hat_y_turned, hat_z, hat_z_turned, hat_x, hat_x_turned = hats

    slots = blocks * BQ
    mine, scales = pl.pallas_call(
        prepare_kernel,
        out_shape=[
            jax.ShapeDtypeStruct((blocks, 4, BQ), f32),
            jax.ShapeDtypeStruct((8, 128), f32),
        ],
        in_specs=[hbm] * 7,
        out_specs=[vmem] * 2,
        scratch_shapes=[
            pltpu.VMEM((3, 1, slots), jnp.int32),
            pltpu.VMEM((3, slots), f32),
            pltpu.VMEM((1, slots), f32),
            pltpu.SMEM((LEVELS,), f32),
            pltpu.SMEM((blocks,), jnp.int32),
            pltpu.SemaphoreType.DMA((7,)),
        ],
        compiler_params=params,
        name="prepare",
    )(
        cell_x.reshape(1, slots),
        cell_y.reshape(1, slots),
        cell_z.reshape(1, slots),
        offsets,
        charge.reshape(1, slots),
        block_count,
        level_amplitude,
    )

    starts = jnp.stack([lax.axis_index(axis) for axis in axes]).astype(jnp.int32)
    grid_shape = jax.ShapeDtypeStruct((plan.total, plan.width), f32)

    def spread(charges, before, turned):
        count = charges.shape[0]
        together = math.gcd(count, 4)
        deep = together * BQ
        first, last = before is None, turned is not None
        operands = [starts, charges] + [x for x in (before, turned) if x is not None]
        return pl.pallas_call(
            lambda *refs: spread_kernel(plan, together, first, last, *refs),
            out_shape=[grid_shape] + [jax.ShapeDtypeStruct((8, plan.width), f32)] * last,
            in_specs=[smem] + [vmem] * (len(operands) - 1),
            out_specs=[vmem] * (1 + last),
            scratch_shapes=[
                pltpu.VMEM((plan.off_x[-1], BQ), f32),
                pltpu.VMEM((plan.off_y[-1], BQ), f32),
                pltpu.VMEM((len(GROUPS), plan.width, deep), bf16),
                pltpu.VMEM((plan.total, deep), bf16),
            ],
            input_output_aliases={} if first else {2: 0},
            cost_estimate=pl.CostEstimate(
                flops=2 * plan.total * 256 * BQ * count, bytes_accessed=0, transcendentals=0
            ),
            compiler_params=params,
            name="spread",
        )(*operands)

    parts = math.gcd(4, rows[0] // 2)
    turned = None
    grids = None
    held = mine
    for number, (axis, pairs) in enumerate(steps):
        got = lax.ppermute(held, axis, pairs)
        held = jnp.concatenate([held, got], axis=0)
        if turned is None:
            turned = pl.pallas_call(
                lambda *refs: turned_kernel(plan, *refs),
                out_shape=grid_shape,
                in_specs=[hbm] + [vmem] * 5,
                out_specs=vmem,
                scratch_shapes=[
                    pltpu.VMEM(rows, f32),
                    pltpu.VMEM((rows[0], plan.stack, rows[2]), f32),
                    pltpu.VMEM((plan.total, rows[2]), f32),
                    pltpu.SemaphoreType.DMA((parts,)),
                ],
                cost_estimate=pl.CostEstimate(
                    flops=2 * 10**9, bytes_accessed=math.prod(rows) * 4, transcendentals=0
                ),
                compiler_params=params,
                name="turned",
            )(density, scales, hat_y_turned, hat_z_turned, hat_x_turned, held)
        new = held if number == 0 else got
        end = number == len(steps) - 1
        out = spread(new, grids, turned if end else None)
        grids = out[0]
    energy = out[1]

    count = rows[0] // parts
    field = None
    for number, (axis, pairs) in enumerate(steps):
        got = lax.ppermute(energy, axis, pairs)
        if number < parts:
            operands = [grids, scales, hat_y, hat_z, hat_x, energy]
            specs = [vmem] * len(operands)
            if field is not None:
                operands.append(field)
                specs.append(hbm)
            field = pl.pallas_call(
                lambda *refs, part=number: field_kernel(plan, part, parts, *refs),
                grid=(1,),
                out_shape=jax.ShapeDtypeStruct(rows, f32),
                in_specs=specs,
                out_specs=pl.BlockSpec(
                    (count, rows[1], rows[2]), lambda i, part=number: (part, 0, 0)
                ),
                scratch_shapes=[pltpu.VMEM((plan.total, rows[2]), f32)],
                input_output_aliases={} if field is None else {len(operands) - 1: 0},
                cost_estimate=pl.CostEstimate(
                    flops=10**9, bytes_accessed=math.prod(rows) * 4 // parts, transcendentals=0
                ),
                compiler_params=params,
                name="field",
            )(*operands)
        energy = energy + got
    fine = math.prod(count * lax.axis_size(axis) for count, axis in zip(rows, axes))
    energy = jnp.sum(energy.reshape(1, -1), axis=1) / fine
    return field, energy


def solution(mesh):
    split_all = ("grp", "slab", "blk", "sub")
    in_specs = (
        P(split_all),
        P(split_all),
        P(split_all),
        P(None, split_all),
        P(split_all),
        P(split_all),
        P(),
        P(("grp", "slab"), "blk", "sub"),
    )
    out_specs = (P(("grp", "slab"), "blk", "sub"), P("grp"))
    return jax.shard_map(
        on_device, mesh=mesh, in_specs=in_specs, out_specs=out_specs, check_vma=False
    )
```

```python
import math
from fractions import Fraction

import jax
import jax.numpy as jnp
from jax import lax
from jax.experimental import pallas as pl
from jax.experimental.pallas import tpu as pltpu
from jax.sharding import PartitionSpec as P

G0X = 64
G0Y = 128
G0Z = 128
BQ = 256
LEVELS = 4
GROUPS = ((0, 1), (2, 3))

spread_width = 1.25
exponent = -0.5 / spread_width**2 * math.log2(math.e)

vmem = pl.BlockSpec(memory_space=pltpu.VMEM)
smem = pl.BlockSpec(memory_space=pltpu.SMEM)
hbm = pl.BlockSpec(memory_space=pltpu.HBM)
params = pltpu.CompilerParams(vmem_limit_bytes=48 * 2**20)


def round_up(value, unit):
    return -(-value // unit) * unit


class Plan:
    def __init__(self, fine, rows):
        self.rows = rows
        self.dims = [
            tuple(base * (LEVELS - level) // LEVELS for base in (G0X, G0Y, G0Z))
            for level in range(LEVELS)
        ]
        self.cells = [
            tuple(dim * part // whole for dim, part, whole in zip(dims, rows, fine))
            for dims in self.dims
        ]
        self.nodes_x = [cells[0] + 1 for cells in self.cells]
        self.main_y = [round_up(cells[1], 16) for cells in self.cells]
        self.pad_x = [round_up(cells[0] + 1, 8) for cells in self.cells]
        self.pad_y = [
            max(main, round_up(cells[1] + 1, 8))
            for main, cells in zip(self.main_y, self.cells)
        ]
        self.pad_z = [round_up(cells[2] + 1, 8) for cells in self.cells]
        self.off_x = [sum(self.pad_x[:level]) for level in range(LEVELS + 1)]
        self.off_y = [sum(self.pad_y[:level]) for level in range(LEVELS + 1)]
        self.off_main = [0]
        for level in range(LEVELS):
            self.off_main.append(
                self.off_main[-1] + self.nodes_x[level] * self.main_y[level]
            )
        self.main_rows = self.off_main[-1]
        self.edge_rows = [
            round_up(self.pad_x[a] + self.pad_x[b], 16) for a, b in GROUPS
        ]
        self.off_edge = []
        at = self.main_rows
        for (a, b), count in zip(GROUPS, self.edge_rows):
            self.off_edge += [at, at + self.pad_x[a]]
            at += count
        self.total = at
        self.off_z = [0, self.pad_z[0], 0, self.pad_z[2]]
        self.width = max(
            round_up(self.pad_z[a] + self.pad_z[b], 128) for a, b in GROUPS
        )
        self.off_stack = [sum(self.main_y[:level]) for level in range(LEVELS + 1)]
        self.stack = round_up(self.off_stack[-1] + 8, 16)

    def main(self, level, node=0, count=1):
        pad = self.main_y[level]
        first = self.off_main[level] + node * pad
        return slice(first, first + count * pad)


def split(value):
    high = value.astype(jnp.bfloat16)
    return high, (value - high.astype(jnp.float32)).astype(jnp.bfloat16)


def dot(left, right, transposed=False):
    return lax.dot_general(
        left,
        right,
        (((1,), (1 if transposed else 0,)), ((), ())),
        preferred_element_type=jnp.float32,
    )


def hat(shape, fine_dim, rows, cells, shift, last):
    point = lax.broadcasted_iota(jnp.int32, shape, fine_dim)
    node = lax.broadcasted_iota(jnp.int32, shape, 1 - fine_dim) - shift
    apart = (node * rows - point * cells).astype(jnp.float32) / rows
    value = jnp.maximum(0.0, 1.0 - jnp.abs(apart))
    return jnp.where((node >= 0) & (node <= last), value, 0.0)


def edge_hat(plan, shape, row_dim):
    row = lax.broadcasted_iota(jnp.int32, shape, row_dim)
    column = lax.broadcasted_iota(jnp.int32, shape, 1 - row_dim)
    value = jnp.zeros(shape, jnp.float32)
    for level in range(LEVELS):
        cells = plan.cells[level][0]
        node = column - (plan.off_edge[level] - plan.main_rows)
        apart = (node * plan.rows[0] - (row >> 3) * cells).astype(jnp.float32)
        one = jnp.maximum(0.0, 1.0 - jnp.abs(apart / plan.rows[0]))
        here = ((row & 7) == level) & (node >= 0) & (node <= cells)
        value = jnp.where(here, one, value)
    return value


def hats_kernel(plan, hat_y, hat_y_turned, hat_z, hat_z_turned, hat_x, hat_x_turned):
    _, rows_y, rows_z = plan.rows
    for turned in (False, True):
        fine_dim = 1 if turned else 0
        parts = []
        edge = 0.0
        for level in range(LEVELS):
            cells = plan.cells[level]
            shape = (rows_y, plan.main_y[level])
            parts.append(
                hat(
                    shape[::-1] if turned else shape, fine_dim, rows_y, cells[1], 0, cells[1] - 1
                )
            )
            shape = (rows_y, plan.stack - plan.off_stack[-1])
            shape = shape[::-1] if turned else shape
            one = hat(shape, fine_dim, rows_y, cells[1], level - cells[1], cells[1])
            column = lax.broadcasted_iota(jnp.int32, shape, 1 - fine_dim)
            edge = edge + jnp.where(column == level, one, 0.0)
            shape = (rows_z, plan.width)
            one = hat(
                shape[::-1] if not turned else shape,
                0 if turned else 1,
                rows_z,
                cells[2],
                plan.off_z[level],
                cells[2],
            ).astype(jnp.bfloat16)
            (hat_z_turned if turned else hat_z)[level] = jnp.concatenate([one, one], axis=0)
        whole = jnp.concatenate(parts + [edge], axis=1 - fine_dim).astype(jnp.bfloat16)
        if turned:
            hat_y_turned[...] = jnp.concatenate([whole, whole], axis=1)
        else:
            hat_y[...] = whole
    hat_x[...] = edge_hat(plan, hat_x.shape, 0).astype(jnp.bfloat16)
    hat_x_turned[...] = edge_hat(plan, hat_x_turned.shape, 1).astype(jnp.bfloat16)


def prepare_kernel(packed, mine, consts):
    blocks = mine.shape[0]
    slot = lax.broadcasted_iota(jnp.int32, (1, BQ), 1).astype(jnp.float32)
    for block in range(blocks):
        columns = slice(block * BQ, (block + 1) * BQ)
        live = packed[5:6, block : block + 1]
        mine[block, 0:1] = jnp.where(slot < live, packed[0:1, columns], 0.0)
        mine[block, 1:4] = packed[1:4, columns]
    shape = (1, consts.shape[1])
    for level in range(LEVELS):
        consts[level : level + 1] = jnp.broadcast_to(packed[4:5, level : level + 1], shape)
    for axis in range(3):
        consts[LEVELS + axis : LEVELS + axis + 1] = jnp.broadcast_to(
            packed[6:7, axis : axis + 1], shape
        )
    consts[LEVELS + 3 :] = jnp.zeros(shape, jnp.float32)


def finish_kernel(scale, energy, got, out):
    total = jnp.sum(energy[...] + got[...], axis=0, keepdims=True)
    out[...] = jnp.sum(total, axis=1, keepdims=True) * scale


def weights(position, first, dim, base, rows):
    place = position * (dim / base)
    nodes = first + lax.broadcasted_iota(jnp.int32, (rows, 1), 0).astype(jnp.float32)
    apart = jnp.abs(nodes - place)
    apart = jnp.minimum(apart, dim - apart)
    return jnp.exp2(apart * apart * exponent)


def spread_kernel(plan, together, first, last, *refs):
    refs = list(refs)
    consts, charges = refs[:2]
    before = None if first else refs[2]
    turned = refs[2 if first else 3] if last else None
    outs = refs[2 + (not first) + last :]
    if last:
        energy = outs.pop(1)
    grids, along_x, along_y, along_z, planes = outs
    begin = [consts[LEVELS + axis : LEVELS + axis + 1, :1] for axis in range(3)]
    steps = charges.shape[0] // together

    def one_step(step, before):
        for number in range(together):
            block = charges[step * together + number]
            columns = slice(number * BQ, (number + 1) * BQ)
            weighted, place_x, place_y, place_z = (block[row : row + 1] for row in range(4))
            for group, levels in enumerate(GROUPS):
                column_z = []
                for level in levels:
                    dims, cells = plan.dims[level], plan.cells[level]
                    along_x[plan.off_x[level] : plan.off_x[level + 1]] = weighted * weights(
                        place_x, begin[0] * cells[0], dims[0], G0X, plan.pad_x[level]
                    )
                    along_y[plan.off_y[level] : plan.off_y[level + 1]] = weights(
                        place_y, begin[1] * cells[1], dims[1], G0Y, plan.pad_y[level]
                    )
                    column_z.append(
                        weights(place_z, begin[2] * cells[2], dims[2], G0Z, plan.pad_z[level])
                    )
                rest = plan.width - sum(plan.pad_z[level] for level in levels)
                if rest:
                    column_z.append(jnp.zeros((rest, BQ), jnp.float32))
                along_z[group, :, columns] = jnp.concatenate(column_z, axis=0).astype(jnp.bfloat16)
                edges = []
                for level in levels:
                    fixed = along_y[plan.off_y[level] : plan.off_y[level] + plan.main_y[level]]
                    for node in range(plan.nodes_x[level]):
                        at = plan.off_x[level] + node
                        planes[plan.main(level, node), columns] = (
                            along_x[at : at + 1] * fixed
                        ).astype(jnp.bfloat16)
                    at = plan.off_y[level] + plan.cells[level][1]
                    edges.append(
                        along_x[plan.off_x[level] : plan.off_x[level + 1]] * along_y[at : at + 1]
                    )
                rest = plan.edge_rows[group] - sum(edge.shape[0] for edge in edges)
                if rest:
                    edges.append(jnp.zeros((rest, BQ), jnp.float32))
                at = plan.off_edge[levels[0]]
                planes[at : at + plan.edge_rows[group], columns] = jnp.concatenate(
                    edges, axis=0
                ).astype(jnp.bfloat16)
        for group, levels in enumerate(GROUPS):
            at = plan.off_edge[levels[0]]
            for rows in [plan.main(level, 0, plan.nodes_x[level]) for level in levels] + [
                slice(at, at + plan.edge_rows[group])
            ]:
                value = dot(planes[rows], along_z[group], transposed=True)
                grids[rows] = value if before is None else before[rows] + value

    one_step(0, before)
    if steps <= 2:
        for step in range(1, steps):
            one_step(step, grids)
    else:
        lax.fori_loop(1, steps, lambda step, _: one_step(step, grids), None)
    if last:
        rows = plan.total // 8
        energy[...] = jnp.sum(
            (grids[...] * turned[...]).reshape(rows, 8, plan.width), axis=0
        )


def hat_terms(points, cells):
    terms = []
    for point in range(points):
        place = Fraction(point * cells, points)
        node = int(place)
        part = float(place - node)
        terms.append([(node, 1.0 - part)] + ([(node + 1, part)] if part else []))
    return terms


def turned_kernel(
    plan, density, scales, hat_y_turned, hat_z_turned, hat_x_turned, unused, out,
    held, along_y, along_x, sems,
):
    rows_x = plan.rows[0]
    parts = sems.shape[0]
    count = rows_x // parts
    copies = [
        pltpu.make_async_copy(
            density.at[pl.ds(part * count, count)],
            held.at[pl.ds(part * count, count)],
            sems.at[part],
        )
        for part in range(parts)
    ]
    for copy in copies:
        copy.start()
    terms = [hat_terms(rows_x, cells[0]) for cells in plan.cells]
    for part in range(parts):
        copies[part].wait()
        for plane in range(part * count, (part + 1) * count, 2):
            both = jnp.concatenate([held[plane], held[plane + 1]], axis=1)
            value = dot(hat_y_turned[...], jnp.concatenate(split(both), axis=0))
            along_y[plane] = value[:, : plan.rows[2]]
            along_y[plane + 1] = value[:, plan.rows[2] :]
    for level in range(LEVELS):
        stack = slice(plan.off_stack[level], plan.off_stack[level + 1])
        for node in range(plan.nodes_x[level]):
            total = None
            for plane in range(rows_x):
                for at, part in terms[level][plane]:
                    if at == node:
                        value = along_y[plane, stack]
                        if part != 1.0:
                            value = value * part
                        total = value if total is None else total + value
            if total is None:
                total = jnp.zeros((plan.main_y[level], plan.rows[2]), jnp.float32)
            along_x[plan.main(level, node)] = total
    first = plan.off_stack[-1]
    edges = jnp.concatenate([along_y[plane, first : first + 8] for plane in range(rows_x)], axis=0)
    high, low = split(edges)
    along_x[plan.main_rows :] = dot(hat_x_turned[...], high) + dot(hat_x_turned[...], low)
    for level in range(LEVELS):
        edge = plan.off_edge[level]
        for rows in (
            plan.main(level, 0, plan.nodes_x[level]),
            slice(edge, edge + plan.pad_x[level]),
        ):
            value = jnp.concatenate(split(along_x[rows]), axis=1)
            out[rows] = dot(value, hat_z_turned[level]) * scales[level : level + 1, :1]
    for group, levels in enumerate(GROUPS):
        at = plan.off_edge[levels[1]] + plan.pad_x[levels[1]]
        end = plan.off_edge[levels[0]] + plan.edge_rows[group]
        if end > at:
            out[at:end] = jnp.zeros((end - at, plan.width), jnp.float32)


def field_kernel(plan, part, parts, *refs):
    grids, scales, hat_y, hat_z, hat_x = refs[:5]
    field, drawn = refs[-2:]
    rows_x = plan.rows[0]
    count = rows_x // parts
    planes = range(part * count, (part + 1) * count)
    terms = [hat_terms(rows_x, cells[0]) for cells in plan.cells]

    def interpolate_z(level, rows):
        value = jnp.concatenate(split(grids[rows] * scales[level : level + 1, : plan.width]), axis=1)
        drawn[rows] = dot(value, hat_z[level])

    for level in range(LEVELS):
        used = [node for plane in planes for node, _ in terms[level][plane]]
        interpolate_z(level, plan.main(level, min(used), max(used) - min(used) + 1))
        edge = plan.off_edge[level]
        interpolate_z(level, slice(edge, edge + plan.pad_x[level]))
    for group, levels in enumerate(GROUPS):
        at = plan.off_edge[levels[1]] + plan.pad_x[levels[1]]
        end = plan.off_edge[levels[0]] + plan.edge_rows[group]
        if end > at:
            drawn[at:end] = jnp.zeros((end - at, drawn.shape[1]), jnp.float32)
    high, low = split(drawn[plan.main_rows :])
    rows = slice(planes[0] * 8, (planes[-1] + 1) * 8)
    edges = dot(hat_x[rows], high) + dot(hat_x[rows], low)
    rest = plan.stack - plan.off_stack[-1] - 8
    for plane in planes[::2]:
        both = []
        for one in (plane, plane + 1):
            stack = []
            for level in range(LEVELS):
                total = None
                for node, weight in terms[level][one]:
                    value = drawn[plan.main(level, node)]
                    if weight != 1.0:
                        value = value * weight
                    total = value if total is None else total + value
                stack.append(total)
            at = (one - planes[0]) * 8
            stack.append(edges[at : at + 8])
            if rest:
                stack.append(jnp.zeros((rest, drawn.shape[1]), jnp.float32))
            both.append(jnp.concatenate(stack, axis=0))
        value = dot(hat_y[...], jnp.concatenate(both, axis=1).astype(jnp.bfloat16))
        field[plane - planes[0]] = value[:, : plan.rows[2]]
        field[plane + 1 - planes[0]] = value[:, plan.rows[2] :]


def rounds(order):
    for axis in order:
        peers = lax.axis_size(axis)
        by = 1
        while by < peers:
            yield axis, [(i, i ^ by) for i in range(peers)]
            by *= 2


def on_device(cell_x, cell_y, cell_z, offsets, charge, block_count, level_amplitude, density):
    blocks = block_count.shape[0]
    rows = density.shape
    axes = ("slab", "blk", "sub")
    plan = Plan(tuple(count * lax.axis_size(axis) for count, axis in zip(rows, axes)), rows)
    order = ("sub", "blk", "slab")
    steps = list(rounds(order))
    f32, bf16 = jnp.float32, jnp.bfloat16

    hats = pl.pallas_call(
        lambda *refs: hats_kernel(plan, *refs),
        out_shape=[
            jax.ShapeDtypeStruct(shape, bf16)
            for shape in (
                (rows[1], plan.stack),
                (plan.stack, 2 * rows[1]),
                (LEVELS, 2 * plan.width, rows[2]),
                (LEVELS, 2 * rows[2], plan.width),
                (rows[0] * 8, plan.total - plan.main_rows),
                (plan.total - plan.main_rows, rows[0] * 8),
            )
        ],
        out_specs=[vmem] * 6,
        compiler_params=params,
        name="hats",
    )()
    hat_y, hat_y_turned, hat_z, hat_z_turned, hat_x, hat_x_turned = hats

    slots = blocks * BQ
    row = lax.broadcasted_iota(jnp.int32, (8, slots), 0)
    column = lax.broadcasted_iota(jnp.int32, (8, slots), 1)

    def wide(vector):
        return jnp.pad(vector.astype(f32), (0, slots - vector.shape[0]))[None, :]

    index = [lax.axis_index(axis).astype(f32) for axis in axes]
    index = jnp.where(column == 0, index[0], jnp.where(column == 1, index[1], index[2]))
    places = jnp.where(row == 1, cell_x[None], jnp.where(row == 2, cell_y[None], cell_z[None]))
    places = places.astype(f32) + jnp.pad(offsets, ((1, 4), (0, 0)))
    packed = jnp.where(
        row == 0,
        charge[None],
        jnp.where(
            row < 4,
            places,
            jnp.where(
                row == 4, wide(level_amplitude), jnp.where(row == 5, wide(block_count), index)
            ),
        ),
    )
    mine, consts = pl.pallas_call(
        prepare_kernel,
        out_shape=[
            jax.ShapeDtypeStruct((blocks, 4, BQ), f32),
            jax.ShapeDtypeStruct((8, 128), f32),
        ],
        in_specs=[vmem],
        out_specs=[vmem] * 2,
        compiler_params=params,
        name="prepare",
    )(packed)

    grid_shape = jax.ShapeDtypeStruct((plan.total, plan.width), f32)

    def spread(charges, before, turned):
        count = charges.shape[0]
        together = math.gcd(count, 4)
        deep = together * BQ
        first, last = before is None, turned is not None
        operands = [consts, charges] + [x for x in (before, turned) if x is not None]
        return pl.pallas_call(
            lambda *refs: spread_kernel(plan, together, first, last, *refs),
            out_shape=[grid_shape] + [jax.ShapeDtypeStruct((8, plan.width), f32)] * last,
            in_specs=[vmem] * len(operands),
            out_specs=[vmem] * (1 + last),
            scratch_shapes=[
                pltpu.VMEM((plan.off_x[-1], BQ), f32),
                pltpu.VMEM((plan.off_y[-1], BQ), f32),
                pltpu.VMEM((len(GROUPS), plan.width, deep), bf16),
                pltpu.VMEM((plan.total, deep), bf16),
            ],
            input_output_aliases={} if first else {2: 0},
            cost_estimate=pl.CostEstimate(
                flops=2 * plan.total * 256 * BQ * count, bytes_accessed=0, transcendentals=0
            ),
            compiler_params=params,
            name="spread",
        )(*operands)

    parts = math.gcd(4, rows[0] // 2)
    turned = None
    grids = None
    held = mine
    for number, (axis, pairs) in enumerate(steps):
        got = lax.ppermute(held, axis, pairs)
        held = jnp.concatenate([held, got], axis=0)
        if turned is None:
            turned = pl.pallas_call(
                lambda *refs: turned_kernel(plan, *refs),
                out_shape=grid_shape,
                in_specs=[hbm] + [vmem] * 5,
                out_specs=vmem,
                scratch_shapes=[
                    pltpu.VMEM(rows, f32),
                    pltpu.VMEM((rows[0], plan.stack, rows[2]), f32),
                    pltpu.VMEM((plan.total, rows[2]), f32),
                    pltpu.SemaphoreType.DMA((parts,)),
                ],
                cost_estimate=pl.CostEstimate(
                    flops=2 * 10**9, bytes_accessed=math.prod(rows) * 4, transcendentals=0
                ),
                compiler_params=pltpu.CompilerParams(vmem_limit_bytes=51 * 2**20),
                name="turned",
            )(density, consts, hat_y_turned, hat_z_turned, hat_x_turned, held)
        new = held if number == 0 else got
        end = number == len(steps) - 1
        out = spread(new, grids, turned if end else None)
        grids = out[0]
    energy = out[1]

    count = rows[0] // parts
    field = None
    for number, (axis, pairs) in enumerate(steps):
        got = lax.ppermute(energy, axis, pairs)
        if number < parts:
            operands = [grids, consts, hat_y, hat_z, hat_x, energy]
            specs = [vmem] * len(operands)
            if field is not None:
                operands.append(field)
                specs.append(hbm)
            field = pl.pallas_call(
                lambda *refs, part=number: field_kernel(plan, part, parts, *refs),
                grid=(1,),
                out_shape=jax.ShapeDtypeStruct(rows, f32),
                in_specs=specs,
                out_specs=pl.BlockSpec(
                    (count, rows[1], rows[2]), lambda i, part=number: (part, 0, 0)
                ),
                scratch_shapes=[pltpu.VMEM((plan.total, rows[2]), f32)],
                input_output_aliases={} if field is None else {len(operands) - 1: 0},
                cost_estimate=pl.CostEstimate(
                    flops=10**9, bytes_accessed=math.prod(rows) * 4 // parts, transcendentals=0
                ),
                compiler_params=params,
                name="field",
            )(*operands)
        if number < len(steps) - 1:
            energy = energy + got
    fine = math.prod(count * lax.axis_size(axis) for count, axis in zip(rows, axes))
    energy = pl.pallas_call(
        lambda *refs: finish_kernel(1.0 / fine, *refs),
        out_shape=jax.ShapeDtypeStruct((1, 1), f32),
        in_specs=[vmem] * 2,
        out_specs=vmem,
        compiler_params=params,
        name="finish",
    )(energy, got)
    return field, energy.reshape(1)


def solution(mesh):
    split_all = ("grp", "slab", "blk", "sub")
    in_specs = (
        P(split_all),
        P(split_all),
        P(split_all),
        P(None, split_all),
        P(split_all),
        P(split_all),
        P(),
        P(("grp", "slab"), "blk", "sub"),
    )
    out_specs = (P(("grp", "slab"), "blk", "sub"), P("grp"))
    return jax.shard_map(
        on_device, mesh=mesh, in_specs=in_specs, out_specs=out_specs, check_vma=False
    )
```

```python
import math
from fractions import Fraction

import jax
import jax.numpy as jnp
from jax import lax
from jax.experimental import pallas as pl
from jax.experimental.pallas import tpu as pltpu
from jax.sharding import PartitionSpec as P

G0X = 64
G0Y = 128
G0Z = 128
BQ = 256
LEVELS = 4
GROUPS = ((0, 1), (2, 3))

SHARES = (0, 0.4, 0.3, 0.3)

spread_width = 1.25
exponent = -0.5 / spread_width**2 * math.log2(math.e)

vmem = pl.BlockSpec(memory_space=pltpu.VMEM)
smem = pl.BlockSpec(memory_space=pltpu.SMEM)
hbm = pl.BlockSpec(memory_space=pltpu.HBM)
params = pltpu.CompilerParams(vmem_limit_bytes=48 * 2**20)


def round_up(value, unit):
    return -(-value // unit) * unit


class Plan:
    def __init__(self, fine, rows):
        self.rows = rows
        self.dims = [
            tuple(base * (LEVELS - level) // LEVELS for base in (G0X, G0Y, G0Z))
            for level in range(LEVELS)
        ]
        self.cells = [
            tuple(dim * part // whole for dim, part, whole in zip(dims, rows, fine))
            for dims in self.dims
        ]
        self.nodes_x = [cells[0] + 1 for cells in self.cells]
        self.main_y = [round_up(cells[1], 16) for cells in self.cells]
        self.pad_x = [round_up(cells[0] + 1, 8) for cells in self.cells]
        self.pad_y = [
            max(main, round_up(cells[1] + 1, 8))
            for main, cells in zip(self.main_y, self.cells)
        ]
        self.pad_z = [round_up(cells[2] + 1, 8) for cells in self.cells]
        self.off_x = [sum(self.pad_x[:level]) for level in range(LEVELS + 1)]
        self.off_y = [sum(self.pad_y[:level]) for level in range(LEVELS + 1)]
        self.off_main = [0]
        for level in range(LEVELS):
            self.off_main.append(
                self.off_main[-1] + self.nodes_x[level] * self.main_y[level]
            )
        self.main_rows = self.off_main[-1]
        self.edge_rows = [
            round_up(self.pad_x[a] + self.pad_x[b], 16) for a, b in GROUPS
        ]
        self.off_edge = []
        at = self.main_rows
        for (a, b), count in zip(GROUPS, self.edge_rows):
            self.off_edge += [at, at + self.pad_x[a]]
            at += count
        self.total = at
        self.off_z = [0, self.pad_z[0], 0, self.pad_z[2]]
        self.width = max(
            round_up(self.pad_z[a] + self.pad_z[b], 128) for a, b in GROUPS
        )
        self.off_stack = [sum(self.main_y[:level]) for level in range(LEVELS + 1)]
        self.stack = round_up(self.off_stack[-1] + 8, 16)

    def main(self, level, node=0, count=1):
        pad = self.main_y[level]
        first = self.off_main[level] + node * pad
        return slice(first, first + count * pad)


def split(value):
    high = value.astype(jnp.bfloat16)
    return high, (value - high.astype(jnp.float32)).astype(jnp.bfloat16)


def dot(left, right, transposed=False):
    return lax.dot_general(
        left,
        right,
        (((1,), (1 if transposed else 0,)), ((), ())),
        preferred_element_type=jnp.float32,
    )


def hat(shape, fine_dim, rows, cells, shift, last):
    point = lax.broadcasted_iota(jnp.int32, shape, fine_dim)
    node = lax.broadcasted_iota(jnp.int32, shape, 1 - fine_dim) - shift
    apart = (node * rows - point * cells).astype(jnp.float32) / rows
    value = jnp.maximum(0.0, 1.0 - jnp.abs(apart))
    return jnp.where((node >= 0) & (node <= last), value, 0.0)


def edge_hat(plan):
    rows_x = plan.rows[0]
    columns = round_up(plan.total - plan.main_rows, 128)
    shape = (rows_x, columns)
    point = lax.broadcasted_iota(jnp.int32, shape, 0)
    column = lax.broadcasted_iota(jnp.int32, shape, 1)
    value = jnp.zeros(shape, jnp.float32)
    shape = (8, columns)
    row = lax.broadcasted_iota(jnp.int32, shape, 0)
    other = lax.broadcasted_iota(jnp.int32, shape, 1)
    mask = jnp.zeros(shape, jnp.float32)
    for level in range(LEVELS):
        cells = plan.cells[level][0]
        first = plan.off_edge[level] - plan.main_rows
        apart = ((column - first) * rows_x - point * cells).astype(jnp.float32) / rows_x
        one = jnp.maximum(0.0, 1.0 - jnp.abs(apart))
        value = jnp.where((column >= first) & (column <= first + cells), one, value)
        here = (row == level) & (other >= first) & (other <= first + cells)
        mask = jnp.where(here, 1.0, mask)
    return (value[:, None, :] * mask[None]).reshape(rows_x * 8, columns)


def hats_kernel(plan, hat_y, hat_y_turned, hat_z, hat_z_turned, hat_x, hat_x_turned):
    _, rows_y, rows_z = plan.rows
    for turned in (False, True):
        fine_dim = 1 if turned else 0
        parts = []
        edge = 0.0
        for level in range(LEVELS):
            cells = plan.cells[level]
            shape = (rows_y, plan.main_y[level])
            parts.append(
                hat(
                    shape[::-1] if turned else shape, fine_dim, rows_y, cells[1], 0, cells[1] - 1
                )
            )
            shape = (rows_y, plan.stack - plan.off_stack[-1])
            shape = shape[::-1] if turned else shape
            one = hat(shape, fine_dim, rows_y, cells[1], level - cells[1], cells[1])
            column = lax.broadcasted_iota(jnp.int32, shape, 1 - fine_dim)
            edge = edge + jnp.where(column == level, one, 0.0)
            shape = (rows_z, plan.width)
            one = hat(
                shape[::-1] if not turned else shape,
                0 if turned else 1,
                rows_z,
                cells[2],
                plan.off_z[level],
                cells[2],
            ).astype(jnp.bfloat16)
            (hat_z_turned if turned else hat_z)[level] = jnp.concatenate([one, one], axis=0)
        whole = jnp.concatenate(parts + [edge], axis=1 - fine_dim).astype(jnp.bfloat16)
        if turned:
            hat_y_turned[...] = jnp.concatenate([whole, whole], axis=1)
        else:
            hat_y[...] = whole
    edges = edge_hat(plan)
    count = plan.total - plan.main_rows
    hat_x[...] = edges[:, :count].astype(jnp.bfloat16)
    hat_x_turned[...] = edges.T[:count].astype(jnp.bfloat16)


def prepare_kernel(raw, mine):
    slot = lax.broadcasted_iota(jnp.int32, (1, BQ), 1).astype(jnp.float32)
    for block in range(mine.shape[0]):
        columns = slice(block * BQ, (block + 1) * BQ)
        live = slot < raw[4:5, block : block + 1]
        mine[block, 0:1] = jnp.where(live, raw[0:1, columns], 0.0)
        mine[block, 1:4] = raw[1:4, columns]


def finish_kernel(scale, energy, got, out):
    total = jnp.sum(energy[...] + got[...], axis=0, keepdims=True)
    out[...] = jnp.sum(total, axis=1, keepdims=True) * scale


def weights(position, first, dim, base, rows):
    place = position * (dim / base)
    nodes = first + lax.broadcasted_iota(jnp.int32, (rows, 1), 0).astype(jnp.float32)
    apart = jnp.abs(nodes - place)
    apart = jnp.minimum(apart, dim - apart)
    return jnp.exp2(apart * apart * exponent)


def fold(value):
    while value.shape[0] > 1:
        half = value.shape[0] // 2
        both = value[:half] + value[half : 2 * half]
        if value.shape[0] % 2:
            first = both[:1] + value[2 * half :]
            both = jnp.concatenate([first, both[1:]], axis=0) if half > 1 else first
        value = both
    return value[0]


def spread_kernel(plan, together, first, last, *refs):
    refs = list(refs)
    index, charges = refs[:2]
    before = None if first else refs[2]
    turned = refs[2 if first else 3] if last else None
    outs = refs[2 + (not first) + last :]
    if last:
        energy = outs.pop(1)
    grids, along_x, along_y, along_z, planes = outs
    begin = [index[axis : axis + 1, :1] for axis in range(3)]
    steps = charges.shape[0] // together

    def one_step(step, before):
        for number in range(together):
            block = charges[step * together + number]
            columns = slice(number * BQ, (number + 1) * BQ)
            weighted, place_x, place_y, place_z = (block[row : row + 1] for row in range(4))
            for group, levels in enumerate(GROUPS):
                column_z = []
                for level in levels:
                    dims, cells = plan.dims[level], plan.cells[level]
                    along_x[plan.off_x[level] : plan.off_x[level + 1]] = weighted * weights(
                        place_x, begin[0] * cells[0], dims[0], G0X, plan.pad_x[level]
                    )
                    along_y[plan.off_y[level] : plan.off_y[level + 1]] = weights(
                        place_y, begin[1] * cells[1], dims[1], G0Y, plan.pad_y[level]
                    )
                    column_z.append(
                        weights(place_z, begin[2] * cells[2], dims[2], G0Z, plan.pad_z[level])
                    )
                rest = plan.width - sum(plan.pad_z[level] for level in levels)
                if rest:
                    column_z.append(jnp.zeros((rest, BQ), jnp.float32))
                along_z[group, :, columns] = jnp.concatenate(column_z, axis=0).astype(jnp.bfloat16)
                edges = []
                for level in levels:
                    fixed = along_y[plan.off_y[level] : plan.off_y[level] + plan.main_y[level]]
                    for node in range(plan.nodes_x[level]):
                        at = plan.off_x[level] + node
                        planes[plan.main(level, node), columns] = (
                            along_x[at : at + 1] * fixed
                        ).astype(jnp.bfloat16)
                    at = plan.off_y[level] + plan.cells[level][1]
                    edges.append(
                        along_x[plan.off_x[level] : plan.off_x[level + 1]] * along_y[at : at + 1]
                    )
                rest = plan.edge_rows[group] - sum(edge.shape[0] for edge in edges)
                if rest:
                    edges.append(jnp.zeros((rest, BQ), jnp.float32))
                at = plan.off_edge[levels[0]]
                planes[at : at + plan.edge_rows[group], columns] = jnp.concatenate(
                    edges, axis=0
                ).astype(jnp.bfloat16)
        for group, levels in enumerate(GROUPS):
            at = plan.off_edge[levels[0]]
            for rows in [plan.main(level, 0, plan.nodes_x[level]) for level in levels] + [
                slice(at, at + plan.edge_rows[group])
            ]:
                value = dot(planes[rows], along_z[group], transposed=True)
                grids[rows] = value if before is None else before[rows] + value

    one_step(0, before)
    if steps <= 2:
        for step in range(1, steps):
            one_step(step, grids)
    else:
        lax.fori_loop(1, steps, lambda step, _: one_step(step, grids), None)
    if last:
        energy[...] = fold((grids[...] * turned[...]).reshape(-1, 8, plan.width))


def hat_terms(points, cells):
    terms = []
    for point in range(points):
        place = Fraction(point * cells, points)
        node = int(place)
        part = float(place - node)
        terms.append([(node, 1.0 - part)] + ([(node + 1, part)] if part else []))
    return terms


def turned_kernel(
    plan, density, amplitude, hat_y_turned, hat_z_turned, hat_x_turned, unused, out,
    held, along_y, along_x, sems,
):
    rows_x = plan.rows[0]
    parts = sems.shape[0]
    count = rows_x // parts
    copies = [
        pltpu.make_async_copy(
            density.at[pl.ds(part * count, count)],
            held.at[pl.ds(part * count, count)],
            sems.at[part],
        )
        for part in range(parts)
    ]
    for copy in copies:
        copy.start()
    terms = [hat_terms(rows_x, cells[0]) for cells in plan.cells]
    for part in range(parts):
        copies[part].wait()
        for plane in range(part * count, (part + 1) * count, 2):
            both = jnp.concatenate([held[plane], held[plane + 1]], axis=1)
            value = dot(hat_y_turned[...], jnp.concatenate(split(both), axis=0))
            along_y[plane] = value[:, : plan.rows[2]]
            along_y[plane + 1] = value[:, plan.rows[2] :]
    for level in range(LEVELS):
        stack = slice(plan.off_stack[level], plan.off_stack[level + 1])
        for node in range(plan.nodes_x[level]):
            total = None
            for plane in range(rows_x):
                for at, part in terms[level][plane]:
                    if at == node:
                        value = along_y[plane, stack]
                        if part != 1.0:
                            value = value * part
                        total = value if total is None else total + value
            if total is None:
                total = jnp.zeros((plan.main_y[level], plan.rows[2]), jnp.float32)
            along_x[plan.main(level, node)] = total
    first = plan.off_stack[-1]
    edges = jnp.concatenate([along_y[plane, first : first + 8] for plane in range(rows_x)], axis=0)
    high, low = split(edges)
    along_x[plan.main_rows :] = dot(hat_x_turned[...], high) + dot(hat_x_turned[...], low)
    for level in range(LEVELS):
        edge = plan.off_edge[level]
        for rows in (
            plan.main(level, 0, plan.nodes_x[level]),
            slice(edge, edge + plan.pad_x[level]),
        ):
            value = jnp.concatenate(split(along_x[rows]), axis=1)
            out[rows] = dot(value, hat_z_turned[level]) * amplitude[:, level : level + 1]
    for group, levels in enumerate(GROUPS):
        at = plan.off_edge[levels[1]] + plan.pad_x[levels[1]]
        end = plan.off_edge[levels[0]] + plan.edge_rows[group]
        if end > at:
            out[at:end] = jnp.zeros((end - at, plan.width), jnp.float32)


def field_kernel(plan, planes, chunk, *refs):
    grids, amplitude, hat_y, hat_z, hat_x = refs[:5]
    field, drawn, held, sems = refs[-4:]
    terms = [hat_terms(plan.rows[0], cells[0]) for cells in plan.cells]

    def interpolate_z(level, rows):
        value = jnp.concatenate(split(grids[rows] * amplitude[:, level : level + 1]), axis=1)
        drawn[rows] = dot(value, hat_z[level])

    for level in range(LEVELS):
        used = [node for plane in planes for node, _ in terms[level][plane]]
        interpolate_z(level, plan.main(level, min(used), max(used) - min(used) + 1))
        edge = plan.off_edge[level]
        interpolate_z(level, slice(edge, edge + plan.pad_x[level]))
    for group, levels in enumerate(GROUPS):
        at = plan.off_edge[levels[1]] + plan.pad_x[levels[1]]
        end = plan.off_edge[levels[0]] + plan.edge_rows[group]
        if end > at:
            drawn[at:end] = jnp.zeros((end - at, drawn.shape[1]), jnp.float32)
    high, low = split(drawn[plan.main_rows :])
    rows = slice(planes[0] * 8, (planes[-1] + 1) * 8)
    edges = dot(hat_x[rows], high) + dot(hat_x[rows], low)
    rest = plan.stack - plan.off_stack[-1] - 8
    copies = []
    for plane in planes[::2]:
        both = []
        for one in (plane, plane + 1):
            stack = []
            for level in range(LEVELS):
                total = None
                for node, weight in terms[level][one]:
                    value = drawn[plan.main(level, node)]
                    if weight != 1.0:
                        value = value * weight
                    total = value if total is None else total + value
                stack.append(total)
            at = (one - planes[0]) * 8
            stack.append(edges[at : at + 8])
            if rest:
                stack.append(jnp.zeros((rest, drawn.shape[1]), jnp.float32))
            both.append(jnp.concatenate(stack, axis=0))
        value = dot(hat_y[...], jnp.concatenate(both, axis=1).astype(jnp.bfloat16))
        at = plane - planes[0]
        held[at] = value[:, : plan.rows[2]]
        held[at + 1] = value[:, plan.rows[2] :]
        at += 2
        if at % chunk == 0 or at == len(planes):
            size = chunk if at % chunk == 0 else at % chunk
            copy = pltpu.make_async_copy(
                held.at[pl.ds(at - size, size)],
                field.at[pl.ds(planes[0] + at - size, size)],
                sems.at[len(copies)],
            )
            copy.start()
            copies.append(copy)
    for copy in copies:
        copy.wait()


def rounds():
    cores = lax.axis_size("sub")
    yield "sub", [(core, core ^ 1) for core in range(cores)]
    for axis in ("blk", "slab"):
        chips = lax.axis_size(axis)
        by = 1
        while by < chips:
            yield (axis, "sub"), [
                (chip * cores + core, (chip ^ by) * cores + (core ^ 1))
                for chip in range(chips)
                for core in range(cores)
            ]
            by *= 2


def on_device(cell_x, cell_y, cell_z, offsets, charge, block_count, level_amplitude, density):
    blocks = block_count.shape[0]
    rows = density.shape
    axes = ("slab", "blk", "sub")
    plan = Plan(tuple(count * lax.axis_size(axis) for count, axis in zip(rows, axes)), rows)
    steps = list(rounds())
    f32, bf16 = jnp.float32, jnp.bfloat16

    hats = pl.pallas_call(
        lambda *refs: hats_kernel(plan, *refs),
        out_shape=[
            jax.ShapeDtypeStruct(shape, bf16)
            for shape in (
                (rows[1], plan.stack),
                (plan.stack, 2 * rows[1]),
                (LEVELS, 2 * plan.width, rows[2]),
                (LEVELS, 2 * rows[2], plan.width),
                (rows[0] * 8, plan.total - plan.main_rows),
                (plan.total - plan.main_rows, rows[0] * 8),
            )
        ],
        out_specs=[vmem] * 6,
        cost_estimate=pl.CostEstimate(flops=15 * 10**8, bytes_accessed=0, transcendentals=0),
        compiler_params=params,
        name="hats",
    )()
    hat_y, hat_y_turned, hat_z, hat_z_turned, hat_x, hat_x_turned = hats
    amplitude = level_amplitude.reshape(1, LEVELS)

    slots = blocks * BQ
    row = lax.broadcasted_iota(jnp.int32, (8, slots), 0)
    counts = lax.dynamic_update_slice(jnp.zeros((slots,), jnp.int32), block_count, (0,))
    whole = jnp.where(row == 1, cell_x[None], jnp.where(row == 2, cell_y[None], cell_z[None]))
    whole = jnp.where(row == 4, counts[None], whole)
    raw = whole.astype(f32) + jnp.pad(offsets, ((1, 4), (0, 0)))
    raw = jnp.where(row == 0, charge[None], raw)
    mine = pl.pallas_call(
        prepare_kernel,
        out_shape=jax.ShapeDtypeStruct((blocks, 4, BQ), f32),
        in_specs=[vmem],
        out_specs=vmem,
        cost_estimate=pl.CostEstimate(flops=15 * 10**8, bytes_accessed=0, transcendentals=0),
        compiler_params=params,
        name="prepare",
    )(raw)
    index = [lax.axis_index(axis).astype(f32) for axis in axes]
    row = lax.broadcasted_iota(jnp.int32, (8, 128), 0)
    begin = jnp.where(row == 0, index[0], jnp.where(row == 1, index[1], index[2]))

    grid_shape = jax.ShapeDtypeStruct((plan.total, plan.width), f32)

    def spread(charges, before, turned):
        count = charges.shape[0]
        together = math.gcd(count, 4)
        deep = together * BQ
        first, last = before is None, turned is not None
        operands = [begin, charges] + [x for x in (before, turned) if x is not None]
        return pl.pallas_call(
            lambda *refs: spread_kernel(plan, together, first, last, *refs),
            out_shape=[grid_shape] + [jax.ShapeDtypeStruct((8, plan.width), f32)] * last,
            in_specs=[vmem] * len(operands),
            out_specs=[vmem] * (1 + last),
            scratch_shapes=[
                pltpu.VMEM((plan.off_x[-1], BQ), f32),
                pltpu.VMEM((plan.off_y[-1], BQ), f32),
                pltpu.VMEM((len(GROUPS), plan.width, deep), bf16),
                pltpu.VMEM((plan.total, deep), bf16),
            ],
            input_output_aliases={} if first else {2: 0},
            cost_estimate=pl.CostEstimate(
                flops=2 * plan.total * 256 * BQ * count, bytes_accessed=0, transcendentals=0
            ),
            compiler_params=params,
            name="spread",
        )(*operands)

    def draw(grids, energy, field, planes):
        operands = [grids, amplitude, hat_y, hat_z, hat_x, energy]
        specs = [vmem] * len(operands)
        if field is not None:
            operands.append(field)
            specs.append(hbm)
        chunk = 8
        return pl.pallas_call(
            lambda *refs: field_kernel(plan, planes, chunk, *refs),
            out_shape=jax.ShapeDtypeStruct(rows, f32),
            in_specs=specs,
            out_specs=hbm,
            scratch_shapes=[
                pltpu.VMEM((plan.total, rows[2]), f32),
                pltpu.VMEM((len(planes), rows[1], rows[2]), f32),
                pltpu.SemaphoreType.DMA((-(-len(planes) // chunk),)),
            ],
            input_output_aliases={} if field is None else {len(operands) - 1: 0},
            cost_estimate=pl.CostEstimate(
                flops=10**9,
                bytes_accessed=len(planes) * rows[1] * rows[2] * 4,
                transcendentals=0,
            ),
            compiler_params=params,
            name="field",
        )(*operands)

    parts = math.gcd(4, rows[0] // 2)
    turned = None
    grids = None
    held = mine
    for number, (axis, pairs) in enumerate(steps):
        got = lax.ppermute(held, axis, pairs)
        held = jnp.concatenate([held, got], axis=0)
        if turned is None:
            turned = pl.pallas_call(
                lambda *refs: turned_kernel(plan, *refs),
                out_shape=grid_shape,
                in_specs=[hbm] + [vmem] * 5,
                out_specs=vmem,
                scratch_shapes=[
                    pltpu.VMEM(rows, f32),
                    pltpu.VMEM((rows[0], plan.stack, rows[2]), f32),
                    pltpu.VMEM((plan.total, rows[2]), f32),
                    pltpu.SemaphoreType.DMA((parts,)),
                ],
                cost_estimate=pl.CostEstimate(
                    flops=2 * 10**9, bytes_accessed=math.prod(rows) * 4, transcendentals=0
                ),
                compiler_params=pltpu.CompilerParams(vmem_limit_bytes=48 * 2**20),
                name="turned",
            )(density, amplitude, hat_y_turned, hat_z_turned, hat_x_turned, held)
        if number:
            end = number == len(steps) - 1
            out = spread(held if number == 1 else got, grids, turned if end else None)
            grids = out[0]
    energy = out[1]

    field = None
    bounds = [0]
    for number in range(len(steps)):
        done = 1.0 if number == len(steps) - 1 else sum(SHARES[: number + 1])
        bounds.append(2 * round(rows[0] // 2 * min(done, 1.0)))
    for number, (axis, pairs) in enumerate(steps):
        got = lax.ppermute(energy, axis, pairs)
        if bounds[number] < bounds[number + 1]:
            planes = range(bounds[number], bounds[number + 1])
            field = draw(grids, energy, field, planes)
        if number < len(steps) - 1:
            energy = energy + got
    fine = math.prod(count * lax.axis_size(axis) for count, axis in zip(rows, axes))
    energy = pl.pallas_call(
        lambda *refs: finish_kernel(1.0 / fine, *refs),
        out_shape=jax.ShapeDtypeStruct((1, 1), f32),
        in_specs=[vmem] * 2,
        out_specs=vmem,
        compiler_params=params,
        name="finish",
    )(energy, got)
    return field, energy.reshape(1)


def solution(mesh):
    split_all = ("grp", "slab", "blk", "sub")
    in_specs = (
        P(split_all),
        P(split_all),
        P(split_all),
        P(None, split_all),
        P(split_all),
        P(split_all),
        P(),
        P(("grp", "slab"), "blk", "sub"),
    )
    out_specs = (P(("grp", "slab"), "blk", "sub"), P("grp"))
    return jax.shard_map(
        on_device, mesh=mesh, in_specs=in_specs, out_specs=out_specs, check_vma=False
    )
```

```python
import math
from fractions import Fraction

import jax
import jax.numpy as jnp
from jax import lax
from jax.experimental import pallas as pl
from jax.experimental.pallas import tpu as pltpu
from jax.sharding import PartitionSpec as P

G0X = 64
G0Y = 128
G0Z = 128
BQ = 256
LEVELS = 4
GROUPS = ((0, 1), (2, 3))


SHARES = (0, 0.5, 0.25, 0.25)

spread_width = 1.25
exponent = -0.5 / spread_width**2 * math.log2(math.e)

vmem = pl.BlockSpec(memory_space=pltpu.VMEM)
smem = pl.BlockSpec(memory_space=pltpu.SMEM)
hbm = pl.BlockSpec(memory_space=pltpu.HBM)
params = pltpu.CompilerParams(vmem_limit_bytes=48 * 2**20)


def round_up(value, unit):
    return -(-value // unit) * unit


class Plan:
    def __init__(self, fine, rows):
        self.rows = rows
        self.dims = [
            tuple(base * (LEVELS - level) // LEVELS for base in (G0X, G0Y, G0Z))
            for level in range(LEVELS)
        ]
        self.cells = [
            tuple(dim * part // whole for dim, part, whole in zip(dims, rows, fine))
            for dims in self.dims
        ]
        self.nodes_x = [cells[0] + 1 for cells in self.cells]
        self.main_y = [round_up(cells[1], 16) for cells in self.cells]
        self.pad_x = [round_up(cells[0] + 1, 8) for cells in self.cells]
        self.pad_y = [
            max(main, round_up(cells[1] + 1, 8))
            for main, cells in zip(self.main_y, self.cells)
        ]
        self.pad_z = [round_up(cells[2] + 1, 8) for cells in self.cells]
        self.off_x = [sum(self.pad_x[:level]) for level in range(LEVELS + 1)]
        self.off_y = [sum(self.pad_y[:level]) for level in range(LEVELS + 1)]
        self.off_main = [0]
        for level in range(LEVELS):
            self.off_main.append(
                self.off_main[-1] + self.nodes_x[level] * self.main_y[level]
            )
        self.main_rows = self.off_main[-1]
        self.edge_rows = [
            round_up(self.pad_x[a] + self.pad_x[b], 16) for a, b in GROUPS
        ]
        self.off_edge = []
        at = self.main_rows
        for (a, b), count in zip(GROUPS, self.edge_rows):
            self.off_edge += [at, at + self.pad_x[a]]
            at += count
        self.total = at
        self.off_z = [0, self.pad_z[0], 0, self.pad_z[2]]
        self.width = max(
            round_up(self.pad_z[a] + self.pad_z[b], 128) for a, b in GROUPS
        )
        self.off_stack = [sum(self.main_y[:level]) for level in range(LEVELS + 1)]
        self.stack = round_up(self.off_stack[-1] + 8, 16)

    def main(self, level, node=0, count=1):
        pad = self.main_y[level]
        first = self.off_main[level] + node * pad
        return slice(first, first + count * pad)


def split(value):
    high = value.astype(jnp.bfloat16)
    return high, (value - high.astype(jnp.float32)).astype(jnp.bfloat16)


def dot(left, right, transposed=False):
    return lax.dot_general(
        left,
        right,
        (((1,), (1 if transposed else 0,)), ((), ())),
        preferred_element_type=jnp.float32,
    )


def hat(shape, fine_dim, rows, cells, shift, last):
    point = lax.broadcasted_iota(jnp.int32, shape, fine_dim)
    node = lax.broadcasted_iota(jnp.int32, shape, 1 - fine_dim) - shift
    apart = (node * rows - point * cells).astype(jnp.float32) / rows
    value = jnp.maximum(0.0, 1.0 - jnp.abs(apart))
    return jnp.where((node >= 0) & (node <= last), value, 0.0)


def edge_hat(plan):
    rows_x = plan.rows[0]
    columns = round_up(plan.total - plan.main_rows, 128)
    shape = (rows_x, columns)
    point = lax.broadcasted_iota(jnp.int32, shape, 0)
    column = lax.broadcasted_iota(jnp.int32, shape, 1)
    value = jnp.zeros(shape, jnp.float32)
    shape = (8, columns)
    row = lax.broadcasted_iota(jnp.int32, shape, 0)
    other = lax.broadcasted_iota(jnp.int32, shape, 1)
    mask = jnp.zeros(shape, jnp.float32)
    for level in range(LEVELS):
        cells = plan.cells[level][0]
        first = plan.off_edge[level] - plan.main_rows
        apart = ((column - first) * rows_x - point * cells).astype(jnp.float32) / rows_x
        one = jnp.maximum(0.0, 1.0 - jnp.abs(apart))
        value = jnp.where((column >= first) & (column <= first + cells), one, value)
        here = (row == level) & (other >= first) & (other <= first + cells)
        mask = jnp.where(here, 1.0, mask)
    return (value[:, None, :] * mask[None]).reshape(rows_x * 8, columns)


def hats_kernel(plan, hat_y, hat_y_turned, hat_z, hat_z_turned, hat_x, hat_x_turned):
    _, rows_y, rows_z = plan.rows
    for turned in (False, True):
        fine_dim = 1 if turned else 0
        parts = []
        edge = 0.0
        for level in range(LEVELS):
            cells = plan.cells[level]
            shape = (rows_y, plan.main_y[level])
            parts.append(
                hat(
                    shape[::-1] if turned else shape, fine_dim, rows_y, cells[1], 0, cells[1] - 1
                )
            )
            shape = (rows_y, plan.stack - plan.off_stack[-1])
            shape = shape[::-1] if turned else shape
            one = hat(shape, fine_dim, rows_y, cells[1], level - cells[1], cells[1])
            column = lax.broadcasted_iota(jnp.int32, shape, 1 - fine_dim)
            edge = edge + jnp.where(column == level, one, 0.0)
            shape = (rows_z, plan.width)
            one = hat(
                shape[::-1] if not turned else shape,
                0 if turned else 1,
                rows_z,
                cells[2],
                plan.off_z[level],
                cells[2],
            ).astype(jnp.bfloat16)
            (hat_z_turned if turned else hat_z)[level] = jnp.concatenate([one, one], axis=0)
        whole = jnp.concatenate(parts + [edge], axis=1 - fine_dim).astype(jnp.bfloat16)
        if turned:
            hat_y_turned[...] = jnp.concatenate([whole, whole], axis=1)
        else:
            hat_y[...] = whole
    edges = edge_hat(plan)
    count = plan.total - plan.main_rows
    hat_x[...] = edges[:, :count].astype(jnp.bfloat16)
    hat_x_turned[...] = edges.T[:count].astype(jnp.bfloat16)


def prepare_kernel(raw, mine):
    slot = lax.broadcasted_iota(jnp.int32, (1, BQ), 1).astype(jnp.float32)
    for block in range(mine.shape[0]):
        columns = slice(block * BQ, (block + 1) * BQ)
        live = slot < raw[4:5, block : block + 1]
        mine[block, 0:1] = jnp.where(live, raw[0:1, columns], 0.0)
        mine[block, 1:4] = raw[1:4, columns]


def finish_kernel(scale, energy, got, out):
    total = jnp.sum(energy[...] + got[...], axis=0, keepdims=True)
    out[...] = jnp.sum(total, axis=1, keepdims=True) * scale


def weights(position, first, dim, base, rows):
    place = position * (dim / base)
    nodes = first + lax.broadcasted_iota(jnp.int32, (rows, 1), 0).astype(jnp.float32)
    apart = jnp.abs(nodes - place)
    apart = jnp.minimum(apart, dim - apart)
    return jnp.exp2(apart * apart * exponent)


def fold(value):
    while value.shape[0] > 1:
        half = value.shape[0] // 2
        both = value[:half] + value[half : 2 * half]
        if value.shape[0] % 2:
            first = both[:1] + value[2 * half :]
            both = jnp.concatenate([first, both[1:]], axis=0) if half > 1 else first
        value = both
    return value[0]


def spread_kernel(plan, together, first, last, *refs):
    refs = list(refs)
    index, charges = refs[:2]
    before = None if first else refs[2]
    turned = refs[2 if first else 3] if last else None
    outs = refs[2 + (not first) + last :]
    if last:
        energy = outs.pop(1)
    grids, along_x, along_y, along_z, planes = outs
    begin = [index[axis : axis + 1, :1] for axis in range(3)]
    steps = charges.shape[0] // together

    def one_step(step, before):
        for number in range(together):
            block = charges[step * together + number]
            columns = slice(number * BQ, (number + 1) * BQ)
            weighted, place_x, place_y, place_z = (block[row : row + 1] for row in range(4))
            for group, levels in enumerate(GROUPS):
                column_z = []
                for level in levels:
                    dims, cells = plan.dims[level], plan.cells[level]
                    along_x[plan.off_x[level] : plan.off_x[level + 1]] = weighted * weights(
                        place_x, begin[0] * cells[0], dims[0], G0X, plan.pad_x[level]
                    )
                    along_y[plan.off_y[level] : plan.off_y[level + 1]] = weights(
                        place_y, begin[1] * cells[1], dims[1], G0Y, plan.pad_y[level]
                    )
                    column_z.append(
                        weights(place_z, begin[2] * cells[2], dims[2], G0Z, plan.pad_z[level])
                    )
                rest = plan.width - sum(plan.pad_z[level] for level in levels)
                if rest:
                    column_z.append(jnp.zeros((rest, BQ), jnp.float32))
                along_z[group, :, columns] = jnp.concatenate(column_z, axis=0).astype(jnp.bfloat16)
                edges = []
                for level in levels:
                    fixed = along_y[plan.off_y[level] : plan.off_y[level] + plan.main_y[level]]
                    for node in range(plan.nodes_x[level]):
                        at = plan.off_x[level] + node
                        planes[plan.main(level, node), columns] = (
                            along_x[at : at + 1] * fixed
                        ).astype(jnp.bfloat16)
                    at = plan.off_y[level] + plan.cells[level][1]
                    edges.append(
                        along_x[plan.off_x[level] : plan.off_x[level + 1]] * along_y[at : at + 1]
                    )
                rest = plan.edge_rows[group] - sum(edge.shape[0] for edge in edges)
                if rest:
                    edges.append(jnp.zeros((rest, BQ), jnp.float32))
                at = plan.off_edge[levels[0]]
                planes[at : at + plan.edge_rows[group], columns] = jnp.concatenate(
                    edges, axis=0
                ).astype(jnp.bfloat16)
        for group, levels in enumerate(GROUPS):
            at = plan.off_edge[levels[0]]
            for rows in [plan.main(level, 0, plan.nodes_x[level]) for level in levels] + [
                slice(at, at + plan.edge_rows[group])
            ]:
                value = dot(planes[rows], along_z[group], transposed=True)
                grids[rows] = value if before is None else before[rows] + value

    one_step(0, before)
    if steps <= 2:
        for step in range(1, steps):
            one_step(step, grids)
    else:
        lax.fori_loop(1, steps, lambda step, _: one_step(step, grids), None)
    if last:
        energy[...] = fold((grids[...] * turned[...]).reshape(-1, 8, plan.width))


def hat_terms(points, cells):
    terms = []
    for point in range(points):
        place = Fraction(point * cells, points)
        node = int(place)
        part = float(place - node)
        terms.append([(node, 1.0 - part)] + ([(node + 1, part)] if part else []))
    return terms


def turned_kernel(
    plan, density, amplitude, hat_y_turned, hat_z_turned, hat_x_turned, unused, out,
    held, along_y, along_x, sems,
):
    rows_x = plan.rows[0]
    parts = sems.shape[0]
    count = rows_x // parts
    copies = [
        pltpu.make_async_copy(
            density.at[pl.ds(part * count, count)],
            held.at[pl.ds(part * count, count)],
            sems.at[part],
        )
        for part in range(parts)
    ]
    for copy in copies:
        copy.start()
    terms = [hat_terms(rows_x, cells[0]) for cells in plan.cells]
    for part in range(parts):
        copies[part].wait()
        for plane in range(part * count, (part + 1) * count, 2):
            both = jnp.concatenate([held[plane], held[plane + 1]], axis=1)
            value = dot(hat_y_turned[...], jnp.concatenate(split(both), axis=0))
            along_y[plane] = value[:, : plan.rows[2]]
            along_y[plane + 1] = value[:, plan.rows[2] :]
    for level in range(LEVELS):
        stack = slice(plan.off_stack[level], plan.off_stack[level + 1])
        for node in range(plan.nodes_x[level]):
            total = None
            for plane in range(rows_x):
                for at, part in terms[level][plane]:
                    if at == node:
                        value = along_y[plane, stack]
                        if part != 1.0:
                            value = value * part
                        total = value if total is None else total + value
            if total is None:
                total = jnp.zeros((plan.main_y[level], plan.rows[2]), jnp.float32)
            along_x[plan.main(level, node)] = total
    first = plan.off_stack[-1]
    edges = jnp.concatenate([along_y[plane, first : first + 8] for plane in range(rows_x)], axis=0)
    high, low = split(edges)
    along_x[plan.main_rows :] = dot(hat_x_turned[...], high) + dot(hat_x_turned[...], low)
    for level in range(LEVELS):
        edge = plan.off_edge[level]
        for rows in (
            plan.main(level, 0, plan.nodes_x[level]),
            slice(edge, edge + plan.pad_x[level]),
        ):
            value = jnp.concatenate(split(along_x[rows]), axis=1)
            out[rows] = dot(value, hat_z_turned[level]) * amplitude[:, level : level + 1]
    for group, levels in enumerate(GROUPS):
        at = plan.off_edge[levels[1]] + plan.pad_x[levels[1]]
        end = plan.off_edge[levels[0]] + plan.edge_rows[group]
        if end > at:
            out[at:end] = jnp.zeros((end - at, plan.width), jnp.float32)


def field_kernel(plan, planes, chunk, *refs):
    grids, amplitude, hat_y, hat_z, hat_x = refs[:5]
    field, drawn, held, sems = refs[-4:]
    terms = [hat_terms(plan.rows[0], cells[0]) for cells in plan.cells]

    def interpolate_z(level, rows):
        value = jnp.concatenate(split(grids[rows] * amplitude[:, level : level + 1]), axis=1)
        drawn[rows] = dot(value, hat_z[level])

    for level in range(LEVELS):
        used = [node for plane in planes for node, _ in terms[level][plane]]
        interpolate_z(level, plan.main(level, min(used), max(used) - min(used) + 1))
        edge = plan.off_edge[level]
        interpolate_z(level, slice(edge, edge + plan.pad_x[level]))
    for group, levels in enumerate(GROUPS):
        at = plan.off_edge[levels[1]] + plan.pad_x[levels[1]]
        end = plan.off_edge[levels[0]] + plan.edge_rows[group]
        if end > at:
            drawn[at:end] = jnp.zeros((end - at, drawn.shape[1]), jnp.float32)
    high, low = split(drawn[plan.main_rows :])
    rows = slice(planes[0] * 8, (planes[-1] + 1) * 8)
    edges = dot(hat_x[rows], high) + dot(hat_x[rows], low)
    rest = plan.stack - plan.off_stack[-1] - 8
    copies = []
    for plane in planes[::2]:
        both = []
        for one in (plane, plane + 1):
            stack = []
            for level in range(LEVELS):
                total = None
                for node, weight in terms[level][one]:
                    value = drawn[plan.main(level, node)]
                    if weight != 1.0:
                        value = value * weight
                    total = value if total is None else total + value
                stack.append(total)
            at = (one - planes[0]) * 8
            stack.append(edges[at : at + 8])
            if rest:
                stack.append(jnp.zeros((rest, drawn.shape[1]), jnp.float32))
            both.append(jnp.concatenate(stack, axis=0))
        value = dot(hat_y[...], jnp.concatenate(both, axis=1).astype(jnp.bfloat16))
        at = plane - planes[0]
        held[at] = value[:, : plan.rows[2]]
        held[at + 1] = value[:, plan.rows[2] :]
        at += 2
        if at % chunk == 0 or at == len(planes):
            size = chunk if at % chunk == 0 else at % chunk
            copy = pltpu.make_async_copy(
                held.at[pl.ds(at - size, size)],
                field.at[pl.ds(planes[0] + at - size, size)],
                sems.at[len(copies)],
            )
            copy.start()
            copies.append(copy)
    for copy in copies:
        copy.wait()


def rounds():
    cores = lax.axis_size("sub")
    found = []
    for axis in ("blk", "slab"):
        by = 1
        while by < lax.axis_size(axis):
            found.append((axis, by))
            by *= 2
    steps = [("sub", [(core, core ^ 1) for core in range(cores)])]
    for axis, by in sorted(found, key=lambda step: -step[1]):
        pairs = [
            (chip * cores + core, (chip ^ by) * cores + (core ^ 1))
            for chip in range(lax.axis_size(axis))
            for core in range(cores)
        ]
        steps.append(((axis, "sub"), pairs))
    return steps


def on_device(cell_x, cell_y, cell_z, offsets, charge, block_count, level_amplitude, density):
    blocks = block_count.shape[0]
    rows = density.shape
    axes = ("slab", "blk", "sub")
    plan = Plan(tuple(count * lax.axis_size(axis) for count, axis in zip(rows, axes)), rows)
    steps = rounds()
    f32, bf16 = jnp.float32, jnp.bfloat16

    hats = pl.pallas_call(
        lambda *refs: hats_kernel(plan, *refs),
        out_shape=[
            jax.ShapeDtypeStruct(shape, bf16)
            for shape in (
                (rows[1], plan.stack),
                (plan.stack, 2 * rows[1]),
                (LEVELS, 2 * plan.width, rows[2]),
                (LEVELS, 2 * rows[2], plan.width),
                (rows[0] * 8, plan.total - plan.main_rows),
                (plan.total - plan.main_rows, rows[0] * 8),
            )
        ],
        out_specs=[vmem] * 6,
        cost_estimate=pl.CostEstimate(flops=15 * 10**8, bytes_accessed=0, transcendentals=0),
        compiler_params=params,
        name="hats",
    )()
    hat_y, hat_y_turned, hat_z, hat_z_turned, hat_x, hat_x_turned = hats
    amplitude = level_amplitude.reshape(1, LEVELS)

    slots = blocks * BQ
    row = lax.broadcasted_iota(jnp.int32, (8, slots), 0)
    counts = lax.dynamic_update_slice(jnp.zeros((slots,), jnp.int32), block_count, (0,))
    whole = jnp.where(row == 1, cell_x[None], jnp.where(row == 2, cell_y[None], cell_z[None]))
    whole = jnp.where(row == 4, counts[None], whole)
    raw = whole.astype(f32) + jnp.pad(offsets, ((1, 4), (0, 0)))
    raw = jnp.where(row == 0, charge[None], raw)
    mine = pl.pallas_call(
        prepare_kernel,
        out_shape=jax.ShapeDtypeStruct((blocks, 4, BQ), f32),
        in_specs=[vmem],
        out_specs=vmem,
        cost_estimate=pl.CostEstimate(flops=15 * 10**8, bytes_accessed=0, transcendentals=0),
        compiler_params=params,
        name="prepare",
    )(raw)
    index = [lax.axis_index(axis).astype(f32) for axis in axes]
    row = lax.broadcasted_iota(jnp.int32, (8, 128), 0)
    begin = jnp.where(row == 0, index[0], jnp.where(row == 1, index[1], index[2]))

    grid_shape = jax.ShapeDtypeStruct((plan.total, plan.width), f32)

    def spread(charges, before, turned):
        count = charges.shape[0]
        together = math.gcd(count, 4)
        deep = together * BQ
        first, last = before is None, turned is not None
        operands = [begin, charges] + [x for x in (before, turned) if x is not None]
        return pl.pallas_call(
            lambda *refs: spread_kernel(plan, together, first, last, *refs),
            out_shape=[grid_shape] + [jax.ShapeDtypeStruct((8, plan.width), f32)] * last,
            in_specs=[vmem] * len(operands),
            out_specs=[vmem] * (1 + last),
            scratch_shapes=[
                pltpu.VMEM((plan.off_x[-1], BQ), f32),
                pltpu.VMEM((plan.off_y[-1], BQ), f32),
                pltpu.VMEM((len(GROUPS), plan.width, deep), bf16),
                pltpu.VMEM((plan.total, deep), bf16),
            ],
            input_output_aliases={} if first else {2: 0},
            cost_estimate=pl.CostEstimate(
                flops=2 * plan.total * 256 * BQ * count, bytes_accessed=0, transcendentals=0
            ),
            compiler_params=params,
            name="spread",
        )(*operands)

    def draw(grids, energy, field, planes):
        operands = [grids, amplitude, hat_y, hat_z, hat_x, energy]
        specs = [vmem] * len(operands)
        if field is not None:
            operands.append(field)
            specs.append(hbm)
        chunk = 8
        return pl.pallas_call(
            lambda *refs: field_kernel(plan, planes, chunk, *refs),
            out_shape=jax.ShapeDtypeStruct(rows, f32),
            in_specs=specs,
            out_specs=hbm,
            scratch_shapes=[
                pltpu.VMEM((plan.total, rows[2]), f32),
                pltpu.VMEM((len(planes), rows[1], rows[2]), f32),
                pltpu.SemaphoreType.DMA((-(-len(planes) // chunk),)),
            ],
            input_output_aliases={} if field is None else {len(operands) - 1: 0},
            cost_estimate=pl.CostEstimate(
                flops=10**9,
                bytes_accessed=len(planes) * rows[1] * rows[2] * 4,
                transcendentals=0,
            ),
            compiler_params=params,
            name="field",
        )(*operands)

    parts = math.gcd(4, rows[0] // 2)
    turned = None
    grids = None
    held = mine
    for number, (axis, pairs) in enumerate(steps):
        got = lax.ppermute(held, axis, pairs)
        held = jnp.concatenate([held, got], axis=0)
        if turned is None:
            turned = pl.pallas_call(
                lambda *refs: turned_kernel(plan, *refs),
                out_shape=grid_shape,
                in_specs=[hbm] + [vmem] * 5,
                out_specs=vmem,
                scratch_shapes=[
                    pltpu.VMEM(rows, f32),
                    pltpu.VMEM((rows[0], plan.stack, rows[2]), f32),
                    pltpu.VMEM((plan.total, rows[2]), f32),
                    pltpu.SemaphoreType.DMA((parts,)),
                ],
                cost_estimate=pl.CostEstimate(
                    flops=2 * 10**9, bytes_accessed=math.prod(rows) * 4, transcendentals=0
                ),
                compiler_params=pltpu.CompilerParams(vmem_limit_bytes=48 * 2**20),
                name="turned",
            )(density, amplitude, hat_y_turned, hat_z_turned, hat_x_turned, held)
        if number:
            end = number == len(steps) - 1
            out = spread(held if number == 1 else got, grids, turned if end else None)
            grids = out[0]
    energy = out[1]

    field = None
    bounds = [0]
    for number in range(len(steps)):
        done = 1.0 if number == len(steps) - 1 else sum(SHARES[: number + 1])
        bounds.append(2 * round(rows[0] // 2 * min(done, 1.0)))
    for number, (axis, pairs) in enumerate(steps):
        got = lax.ppermute(energy, axis, pairs)
        if bounds[number] < bounds[number + 1]:
            planes = range(bounds[number], bounds[number + 1])
            field = draw(grids, energy, field, planes)
        if number < len(steps) - 1:
            energy = energy + got
    fine = math.prod(count * lax.axis_size(axis) for count, axis in zip(rows, axes))
    energy = pl.pallas_call(
        lambda *refs: finish_kernel(1.0 / fine, *refs),
        out_shape=jax.ShapeDtypeStruct((1, 1), f32),
        in_specs=[vmem] * 2,
        out_specs=vmem,
        compiler_params=params,
        name="finish",
    )(energy, got)
    return field, energy.reshape(1)


def solution(mesh):
    split_all = ("grp", "slab", "blk", "sub")
    in_specs = (
        P(split_all),
        P(split_all),
        P(split_all),
        P(None, split_all),
        P(split_all),
        P(split_all),
        P(),
        P(("grp", "slab"), "blk", "sub"),
    )
    out_specs = (P(("grp", "slab"), "blk", "sub"), P("grp"))
    return jax.shard_map(
        on_device, mesh=mesh, in_specs=in_specs, out_specs=out_specs, check_vma=False
    )
```

```python
import math
from fractions import Fraction

import jax
import jax.numpy as jnp
from jax import lax
from jax.experimental import pallas as pl
from jax.experimental.pallas import tpu as pltpu
from jax.sharding import PartitionSpec as P

G0X = 64
G0Y = 128
G0Z = 128
BQ = 256
LEVELS = 4
GROUPS = ((0, 1), (2, 3))


SIZES = (3, 5)
SHARES = (0, 0.5, 0.25, 0.25)

spread_width = 1.25
exponent = -0.5 / spread_width**2 * math.log2(math.e)

vmem = pl.BlockSpec(memory_space=pltpu.VMEM)
smem = pl.BlockSpec(memory_space=pltpu.SMEM)
hbm = pl.BlockSpec(memory_space=pltpu.HBM)
params = pltpu.CompilerParams(vmem_limit_bytes=48 * 2**20)


def round_up(value, unit):
    return -(-value // unit) * unit


class Plan:
    def __init__(self, fine, rows):
        self.rows = rows
        self.dims = [
            tuple(base * (LEVELS - level) // LEVELS for base in (G0X, G0Y, G0Z))
            for level in range(LEVELS)
        ]
        self.cells = [
            tuple(dim * part // whole for dim, part, whole in zip(dims, rows, fine))
            for dims in self.dims
        ]
        self.nodes_x = [cells[0] + 1 for cells in self.cells]
        self.main_y = [round_up(cells[1], 16) for cells in self.cells]
        self.pad_x = [round_up(cells[0] + 1, 8) for cells in self.cells]
        self.pad_y = [
            max(main, round_up(cells[1] + 1, 8))
            for main, cells in zip(self.main_y, self.cells)
        ]
        self.pad_z = [round_up(cells[2] + 1, 8) for cells in self.cells]
        self.off_x = [sum(self.pad_x[:level]) for level in range(LEVELS + 1)]
        self.off_y = [sum(self.pad_y[:level]) for level in range(LEVELS + 1)]
        self.off_main = [0]
        for level in range(LEVELS):
            self.off_main.append(
                self.off_main[-1] + self.nodes_x[level] * self.main_y[level]
            )
        self.main_rows = self.off_main[-1]
        self.edge_rows = [
            round_up(self.pad_x[a] + self.pad_x[b], 16) for a, b in GROUPS
        ]
        self.off_edge = []
        at = self.main_rows
        for (a, b), count in zip(GROUPS, self.edge_rows):
            self.off_edge += [at, at + self.pad_x[a]]
            at += count
        self.total = at
        self.off_z = [0, self.pad_z[0], 0, self.pad_z[2]]
        self.width = max(
            round_up(self.pad_z[a] + self.pad_z[b], 128) for a, b in GROUPS
        )
        self.off_stack = [sum(self.main_y[:level]) for level in range(LEVELS + 1)]
        self.stack = round_up(self.off_stack[-1] + 8, 16)

    def main(self, level, node=0, count=1):
        pad = self.main_y[level]
        first = self.off_main[level] + node * pad
        return slice(first, first + count * pad)


def split(value):
    high = value.astype(jnp.bfloat16)
    return high, (value - high.astype(jnp.float32)).astype(jnp.bfloat16)


def dot(left, right, transposed=False):
    return lax.dot_general(
        left,
        right,
        (((1,), (1 if transposed else 0,)), ((), ())),
        preferred_element_type=jnp.float32,
    )


def hat(shape, fine_dim, rows, cells, shift, last):
    point = lax.broadcasted_iota(jnp.int32, shape, fine_dim)
    node = lax.broadcasted_iota(jnp.int32, shape, 1 - fine_dim) - shift
    apart = (node * rows - point * cells).astype(jnp.float32) / rows
    value = jnp.maximum(0.0, 1.0 - jnp.abs(apart))
    return jnp.where((node >= 0) & (node <= last), value, 0.0)


def edge_hat(plan):
    rows_x = plan.rows[0]
    columns = round_up(plan.total - plan.main_rows, 128)
    shape = (rows_x, columns)
    point = lax.broadcasted_iota(jnp.int32, shape, 0)
    column = lax.broadcasted_iota(jnp.int32, shape, 1)
    value = jnp.zeros(shape, jnp.float32)
    shape = (8, columns)
    row = lax.broadcasted_iota(jnp.int32, shape, 0)
    other = lax.broadcasted_iota(jnp.int32, shape, 1)
    mask = jnp.zeros(shape, jnp.float32)
    for level in range(LEVELS):
        cells = plan.cells[level][0]
        first = plan.off_edge[level] - plan.main_rows
        apart = ((column - first) * rows_x - point * cells).astype(jnp.float32) / rows_x
        one = jnp.maximum(0.0, 1.0 - jnp.abs(apart))
        value = jnp.where((column >= first) & (column <= first + cells), one, value)
        here = (row == level) & (other >= first) & (other <= first + cells)
        mask = jnp.where(here, 1.0, mask)
    return (value[:, None, :] * mask[None]).reshape(rows_x * 8, columns)


def hats_kernel(plan, hat_y, hat_y_turned, hat_z, hat_z_turned, hat_x, hat_x_turned):
    _, rows_y, rows_z = plan.rows
    for turned in (False, True):
        fine_dim = 1 if turned else 0
        parts = []
        edge = 0.0
        for level in range(LEVELS):
            cells = plan.cells[level]
            shape = (rows_y, plan.main_y[level])
            parts.append(
                hat(
                    shape[::-1] if turned else shape, fine_dim, rows_y, cells[1], 0, cells[1] - 1
                )
            )
            shape = (rows_y, plan.stack - plan.off_stack[-1])
            shape = shape[::-1] if turned else shape
            one = hat(shape, fine_dim, rows_y, cells[1], level - cells[1], cells[1])
            column = lax.broadcasted_iota(jnp.int32, shape, 1 - fine_dim)
            edge = edge + jnp.where(column == level, one, 0.0)
            shape = (rows_z, plan.width)
            one = hat(
                shape[::-1] if not turned else shape,
                0 if turned else 1,
                rows_z,
                cells[2],
                plan.off_z[level],
                cells[2],
            ).astype(jnp.bfloat16)
            (hat_z_turned if turned else hat_z)[level] = jnp.concatenate([one, one], axis=0)
        whole = jnp.concatenate(parts + [edge], axis=1 - fine_dim).astype(jnp.bfloat16)
        if turned:
            hat_y_turned[...] = jnp.concatenate([whole, whole], axis=1)
        else:
            hat_y[...] = whole
    edges = edge_hat(plan)
    count = plan.total - plan.main_rows
    hat_x[...] = edges[:, :count].astype(jnp.bfloat16)
    hat_x_turned[...] = edges.T[:count].astype(jnp.bfloat16)


def prepare_kernel(raw, mine):
    slot = lax.broadcasted_iota(jnp.int32, (1, BQ), 1).astype(jnp.float32)
    for block in range(mine.shape[0]):
        columns = slice(block * BQ, (block + 1) * BQ)
        live = slot < raw[4:5, block : block + 1]
        mine[block, 0:1] = jnp.where(live, raw[0:1, columns], 0.0)
        mine[block, 1:4] = raw[1:4, columns]


def finish_kernel(scale, energy, got, out):
    total = jnp.sum(energy[...] + got[...], axis=0, keepdims=True)
    out[...] = jnp.sum(total, axis=1, keepdims=True) * scale


def weights(position, first, dim, base, rows):
    place = position * (dim / base)
    nodes = first + lax.broadcasted_iota(jnp.int32, (rows, 1), 0).astype(jnp.float32)
    apart = jnp.abs(nodes - place)
    apart = jnp.minimum(apart, dim - apart)
    return jnp.exp2(apart * apart * exponent)


def fold(value):
    while value.shape[0] > 1:
        half = value.shape[0] // 2
        both = value[:half] + value[half : 2 * half]
        if value.shape[0] % 2:
            first = both[:1] + value[2 * half :]
            both = jnp.concatenate([first, both[1:]], axis=0) if half > 1 else first
        value = both
    return value[0]


def spread_kernel(plan, sizes, first, last, *refs):
    refs = list(refs)
    index, charges = refs[:2]
    before = None if first else refs[2]
    turned = refs[2 if first else 3] if last else None
    outs = refs[2 + (not first) + last :]
    if last:
        energy = outs.pop(1)
    grids, along_x, along_y, along_z, planes = outs
    begin = [index[axis : axis + 1, :1] for axis in range(3)]
    def one_step(start, together, before):
        for number in range(together):
            block = charges[start + number]
            columns = slice(number * BQ, (number + 1) * BQ)
            weighted, place_x, place_y, place_z = (block[row : row + 1] for row in range(4))
            for group, levels in enumerate(GROUPS):
                column_z = []
                for level in levels:
                    dims, cells = plan.dims[level], plan.cells[level]
                    along_x[plan.off_x[level] : plan.off_x[level + 1]] = weighted * weights(
                        place_x, begin[0] * cells[0], dims[0], G0X, plan.pad_x[level]
                    )
                    along_y[plan.off_y[level] : plan.off_y[level + 1]] = weights(
                        place_y, begin[1] * cells[1], dims[1], G0Y, plan.pad_y[level]
                    )
                    column_z.append(
                        weights(place_z, begin[2] * cells[2], dims[2], G0Z, plan.pad_z[level])
                    )
                rest = plan.width - sum(plan.pad_z[level] for level in levels)
                if rest:
                    column_z.append(jnp.zeros((rest, BQ), jnp.float32))
                along_z[group, :, columns] = jnp.concatenate(column_z, axis=0).astype(jnp.bfloat16)
                edges = []
                for level in levels:
                    fixed = along_y[plan.off_y[level] : plan.off_y[level] + plan.main_y[level]]
                    for node in range(plan.nodes_x[level]):
                        at = plan.off_x[level] + node
                        planes[plan.main(level, node), columns] = (
                            along_x[at : at + 1] * fixed
                        ).astype(jnp.bfloat16)
                    at = plan.off_y[level] + plan.cells[level][1]
                    edges.append(
                        along_x[plan.off_x[level] : plan.off_x[level + 1]] * along_y[at : at + 1]
                    )
                rest = plan.edge_rows[group] - sum(edge.shape[0] for edge in edges)
                if rest:
                    edges.append(jnp.zeros((rest, BQ), jnp.float32))
                at = plan.off_edge[levels[0]]
                planes[at : at + plan.edge_rows[group], columns] = jnp.concatenate(
                    edges, axis=0
                ).astype(jnp.bfloat16)
        for group, levels in enumerate(GROUPS):
            at = plan.off_edge[levels[0]]
            for rows in [plan.main(level, 0, plan.nodes_x[level]) for level in levels] + [
                slice(at, at + plan.edge_rows[group])
            ]:
                deep = together * BQ
                value = dot(planes[rows, :deep], along_z[group, :, :deep], transposed=True)
                grids[rows] = value if before is None else before[rows] + value

    count = sum(sizes)
    for number, size in enumerate(sizes):
        one_step(sum(sizes[:number]), size, grids if number else before)
    rest = (charges.shape[0] - count) // sizes[-1]
    if rest:
        lax.fori_loop(
            0, rest, lambda step, _: one_step(count + step * sizes[-1], sizes[-1], grids), None
        )
    if last:
        energy[...] = fold((grids[...] * turned[...]).reshape(-1, 8, plan.width))


def hat_terms(points, cells):
    terms = []
    for point in range(points):
        place = Fraction(point * cells, points)
        node = int(place)
        part = float(place - node)
        terms.append([(node, 1.0 - part)] + ([(node + 1, part)] if part else []))
    return terms


def turned_kernel(
    plan, density, amplitude, hat_y_turned, hat_z_turned, hat_x_turned, unused, out,
    held, along_y, along_x, sems,
):
    rows_x = plan.rows[0]
    parts = sems.shape[0]
    count = rows_x // parts
    copies = [
        pltpu.make_async_copy(
            density.at[pl.ds(part * count, count)],
            held.at[pl.ds(part * count, count)],
            sems.at[part],
        )
        for part in range(parts)
    ]
    for copy in copies:
        copy.start()
    terms = [hat_terms(rows_x, cells[0]) for cells in plan.cells]
    for part in range(parts):
        copies[part].wait()
        for plane in range(part * count, (part + 1) * count, 2):
            both = jnp.concatenate([held[plane], held[plane + 1]], axis=1)
            value = dot(hat_y_turned[...], jnp.concatenate(split(both), axis=0))
            along_y[plane] = value[:, : plan.rows[2]]
            along_y[plane + 1] = value[:, plan.rows[2] :]
    for level in range(LEVELS):
        stack = slice(plan.off_stack[level], plan.off_stack[level + 1])
        for node in range(plan.nodes_x[level]):
            total = None
            for plane in range(rows_x):
                for at, part in terms[level][plane]:
                    if at == node:
                        value = along_y[plane, stack]
                        if part != 1.0:
                            value = value * part
                        total = value if total is None else total + value
            if total is None:
                total = jnp.zeros((plan.main_y[level], plan.rows[2]), jnp.float32)
            along_x[plan.main(level, node)] = total
    first = plan.off_stack[-1]
    edges = jnp.concatenate([along_y[plane, first : first + 8] for plane in range(rows_x)], axis=0)
    high, low = split(edges)
    along_x[plan.main_rows :] = dot(hat_x_turned[...], high) + dot(hat_x_turned[...], low)
    for level in range(LEVELS):
        edge = plan.off_edge[level]
        for rows in (
            plan.main(level, 0, plan.nodes_x[level]),
            slice(edge, edge + plan.pad_x[level]),
        ):
            value = jnp.concatenate(split(along_x[rows]), axis=1)
            out[rows] = dot(value, hat_z_turned[level]) * amplitude[:, level : level + 1]
    for group, levels in enumerate(GROUPS):
        at = plan.off_edge[levels[1]] + plan.pad_x[levels[1]]
        end = plan.off_edge[levels[0]] + plan.edge_rows[group]
        if end > at:
            out[at:end] = jnp.zeros((end - at, plan.width), jnp.float32)


def field_kernel(plan, planes, chunk, *refs):
    grids, amplitude, hat_y, hat_z, hat_x = refs[:5]
    field, drawn, held, sems = refs[-4:]
    terms = [hat_terms(plan.rows[0], cells[0]) for cells in plan.cells]

    def interpolate_z(level, rows):
        value = jnp.concatenate(split(grids[rows] * amplitude[:, level : level + 1]), axis=1)
        drawn[rows] = dot(value, hat_z[level])

    for level in range(LEVELS):
        used = [node for plane in planes for node, _ in terms[level][plane]]
        interpolate_z(level, plan.main(level, min(used), max(used) - min(used) + 1))
        edge = plan.off_edge[level]
        interpolate_z(level, slice(edge, edge + plan.pad_x[level]))
    for group, levels in enumerate(GROUPS):
        at = plan.off_edge[levels[1]] + plan.pad_x[levels[1]]
        end = plan.off_edge[levels[0]] + plan.edge_rows[group]
        if end > at:
            drawn[at:end] = jnp.zeros((end - at, drawn.shape[1]), jnp.float32)
    high, low = split(drawn[plan.main_rows :])
    rows = slice(planes[0] * 8, (planes[-1] + 1) * 8)
    edges = dot(hat_x[rows], high) + dot(hat_x[rows], low)
    rest = plan.stack - plan.off_stack[-1] - 8
    copies = []
    for plane in planes[::2]:
        both = []
        for one in (plane, plane + 1):
            stack = []
            for level in range(LEVELS):
                total = None
                for node, weight in terms[level][one]:
                    value = drawn[plan.main(level, node)]
                    if weight != 1.0:
                        value = value * weight
                    total = value if total is None else total + value
                stack.append(total)
            at = (one - planes[0]) * 8
            stack.append(edges[at : at + 8])
            if rest:
                stack.append(jnp.zeros((rest, drawn.shape[1]), jnp.float32))
            both.append(jnp.concatenate(stack, axis=0))
        value = dot(hat_y[...], jnp.concatenate(both, axis=1).astype(jnp.bfloat16))
        at = plane - planes[0]
        held[at] = value[:, : plan.rows[2]]
        held[at + 1] = value[:, plan.rows[2] :]
        at += 2
        if at % chunk == 0 or at == len(planes):
            size = chunk if at % chunk == 0 else at % chunk
            copy = pltpu.make_async_copy(
                held.at[pl.ds(at - size, size)],
                field.at[pl.ds(planes[0] + at - size, size)],
                sems.at[len(copies)],
            )
            copy.start()
            copies.append(copy)
    for copy in copies:
        copy.wait()


def rounds():
    cores = lax.axis_size("sub")
    found = []
    for axis in ("blk", "slab"):
        by = 1
        while by < lax.axis_size(axis):
            found.append((axis, by))
            by *= 2
    steps = [("sub", [(core, core ^ 1) for core in range(cores)])]
    for axis, by in sorted(found, key=lambda step: -step[1]):
        pairs = [
            (chip * cores + core, (chip ^ by) * cores + (core ^ 1))
            for chip in range(lax.axis_size(axis))
            for core in range(cores)
        ]
        steps.append(((axis, "sub"), pairs))
    return steps


def on_device(cell_x, cell_y, cell_z, offsets, charge, block_count, level_amplitude, density):
    blocks = block_count.shape[0]
    rows = density.shape
    axes = ("slab", "blk", "sub")
    plan = Plan(tuple(count * lax.axis_size(axis) for count, axis in zip(rows, axes)), rows)
    steps = rounds()
    f32, bf16 = jnp.float32, jnp.bfloat16

    hats = pl.pallas_call(
        lambda *refs: hats_kernel(plan, *refs),
        out_shape=[
            jax.ShapeDtypeStruct(shape, bf16)
            for shape in (
                (rows[1], plan.stack),
                (plan.stack, 2 * rows[1]),
                (LEVELS, 2 * plan.width, rows[2]),
                (LEVELS, 2 * rows[2], plan.width),
                (rows[0] * 8, plan.total - plan.main_rows),
                (plan.total - plan.main_rows, rows[0] * 8),
            )
        ],
        out_specs=[vmem] * 6,
        cost_estimate=pl.CostEstimate(flops=15 * 10**8, bytes_accessed=0, transcendentals=0),
        compiler_params=params,
        name="hats",
    )()
    hat_y, hat_y_turned, hat_z, hat_z_turned, hat_x, hat_x_turned = hats
    amplitude = level_amplitude.reshape(1, LEVELS)

    slots = blocks * BQ
    row = lax.broadcasted_iota(jnp.int32, (8, slots), 0)
    counts = lax.dynamic_update_slice(jnp.zeros((slots,), jnp.int32), block_count, (0,))
    whole = jnp.where(row == 1, cell_x[None], jnp.where(row == 2, cell_y[None], cell_z[None]))
    whole = jnp.where(row == 4, counts[None], whole)
    raw = whole.astype(f32) + jnp.pad(offsets, ((1, 4), (0, 0)))
    raw = jnp.where(row == 0, charge[None], raw)
    mine = pl.pallas_call(
        prepare_kernel,
        out_shape=jax.ShapeDtypeStruct((blocks, 4, BQ), f32),
        in_specs=[vmem],
        out_specs=vmem,
        cost_estimate=pl.CostEstimate(flops=15 * 10**8, bytes_accessed=0, transcendentals=0),
        compiler_params=params,
        name="prepare",
    )(raw)
    index = [lax.axis_index(axis).astype(f32) for axis in axes]
    row = lax.broadcasted_iota(jnp.int32, (8, 128), 0)
    begin = jnp.where(row == 0, index[0], jnp.where(row == 1, index[1], index[2]))

    grid_shape = jax.ShapeDtypeStruct((plan.total, plan.width), f32)

    def spread(charges, before, turned):
        count = charges.shape[0]
        sizes = SIZES if count == 8 else (math.gcd(count, 4),)
        deep = max(sizes) * BQ
        first, last = before is None, turned is not None
        operands = [begin, charges] + [x for x in (before, turned) if x is not None]
        return pl.pallas_call(
            lambda *refs: spread_kernel(plan, sizes, first, last, *refs),
            out_shape=[grid_shape] + [jax.ShapeDtypeStruct((8, plan.width), f32)] * last,
            in_specs=[vmem] * len(operands),
            out_specs=[vmem] * (1 + last),
            scratch_shapes=[
                pltpu.VMEM((plan.off_x[-1], BQ), f32),
                pltpu.VMEM((plan.off_y[-1], BQ), f32),
                pltpu.VMEM((len(GROUPS), plan.width, deep), bf16),
                pltpu.VMEM((plan.total, deep), bf16),
            ],
            input_output_aliases={} if first else {2: 0},
            cost_estimate=pl.CostEstimate(
                flops=2 * plan.total * 256 * BQ * count, bytes_accessed=0, transcendentals=0
            ),
            compiler_params=params,
            name="spread",
        )(*operands)

    def draw(grids, energy, field, planes):
        operands = [grids, amplitude, hat_y, hat_z, hat_x, energy]
        specs = [vmem] * len(operands)
        if field is not None:
            operands.append(field)
            specs.append(hbm)
        chunk = 8
        return pl.pallas_call(
            lambda *refs: field_kernel(plan, planes, chunk, *refs),
            out_shape=jax.ShapeDtypeStruct(rows, f32),
            in_specs=specs,
            out_specs=hbm,
            scratch_shapes=[
                pltpu.VMEM((plan.total, rows[2]), f32),
                pltpu.VMEM((len(planes), rows[1], rows[2]), f32),
                pltpu.SemaphoreType.DMA((-(-len(planes) // chunk),)),
            ],
            input_output_aliases={} if field is None else {len(operands) - 1: 0},
            cost_estimate=pl.CostEstimate(
                flops=10**9,
                bytes_accessed=len(planes) * rows[1] * rows[2] * 4,
                transcendentals=0,
            ),
            compiler_params=params,
            name="field",
        )(*operands)

    parts = math.gcd(4, rows[0] // 2)
    turned = None
    grids = None
    held = mine
    for number, (axis, pairs) in enumerate(steps):
        got = lax.ppermute(held, axis, pairs)
        held = jnp.concatenate([held, got], axis=0)
        if turned is None:
            turned = pl.pallas_call(
                lambda *refs: turned_kernel(plan, *refs),
                out_shape=grid_shape,
                in_specs=[hbm] + [vmem] * 5,
                out_specs=vmem,
                scratch_shapes=[
                    pltpu.VMEM(rows, f32),
                    pltpu.VMEM((rows[0], plan.stack, rows[2]), f32),
                    pltpu.VMEM((plan.total, rows[2]), f32),
                    pltpu.SemaphoreType.DMA((parts,)),
                ],
                cost_estimate=pl.CostEstimate(
                    flops=2 * 10**9, bytes_accessed=math.prod(rows) * 4, transcendentals=0
                ),
                compiler_params=pltpu.CompilerParams(vmem_limit_bytes=48 * 2**20),
                name="turned",
            )(density, amplitude, hat_y_turned, hat_z_turned, hat_x_turned, held)
        if number:
            end = number == len(steps) - 1
            out = spread(held if number == 1 else got, grids, turned if end else None)
            grids = out[0]
    energy = out[1]

    field = None
    bounds = [0]
    for number in range(len(steps)):
        done = 1.0 if number == len(steps) - 1 else sum(SHARES[: number + 1])
        bounds.append(2 * round(rows[0] // 2 * min(done, 1.0)))
    for number, (axis, pairs) in enumerate(steps):
        got = lax.ppermute(energy, axis, pairs)
        if bounds[number] < bounds[number + 1]:
            planes = range(bounds[number], bounds[number + 1])
            field = draw(grids, energy, field, planes)
        if number < len(steps) - 1:
            energy = energy + got
    fine = math.prod(count * lax.axis_size(axis) for count, axis in zip(rows, axes))
    energy = pl.pallas_call(
        lambda *refs: finish_kernel(1.0 / fine, *refs),
        out_shape=jax.ShapeDtypeStruct((1, 1), f32),
        in_specs=[vmem] * 2,
        out_specs=vmem,
        compiler_params=params,
        name="finish",
    )(energy, got)
    return field, energy.reshape(1)


def solution(mesh):
    split_all = ("grp", "slab", "blk", "sub")
    in_specs = (
        P(split_all),
        P(split_all),
        P(split_all),
        P(None, split_all),
        P(split_all),
        P(split_all),
        P(),
        P(("grp", "slab"), "blk", "sub"),
    )
    out_specs = (P(("grp", "slab"), "blk", "sub"), P("grp"))
    return jax.shard_map(
        on_device, mesh=mesh, in_specs=in_specs, out_specs=out_specs, check_vma=False
    )
```
